32 devices in a mesh: dp: 4 (over y, core), seq: 8 (over z, x).
Axes of the slice: x: 2, y: 2, z: 4, core: 2. Of those that a mesh axis runs over, the one named last changes fastest.
Arguments:
- hidden: bfloat16 [2, 8192, 2048], P(None, ('dp', 'seq')), may hold values from -6 to 6
- lengths: int32 [2, 4, 3], P(None, 'dp'), may hold values from 1 to 1024, 2048 in all within a row
- token_order: int32 [2, 4, 2048], P(None, 'dp'), may hold values from 0 to 2047, each once within a row
- norm_gain: bfloat16 [2, 2048], P(None, ('dp', 'seq')), may hold values from 0.099609375 to 1.8984375
- in_weight: bfloat16 [2, 2048, 8512], P(None, ('dp', 'seq')), may hold values from -0.125 to 0.125
- conv_weight: bfloat16 [2, 4, 4352], P(None, None, ('dp', 'seq')), may hold values from -0.5 to 0.5
- conv_bias: bfloat16 [2, 4352], P(None, ('dp', 'seq')), may hold values from -0.5 to 0.5
- dt_bias: float32 [2, 64], P(None, 'seq'), may hold values from -4 to -1
- log_decay: float32 [2, 64], P(None, 'seq'), may hold values from -4 to 2.5
- skip_gain: float32 [2, 64], P(None, 'seq'), may hold values from 0.2 to 3.3
- gate_gain: bfloat16 [2, 4096], P(None, ('dp', 'seq')), may hold values from 0.099609375 to 1.8984375
- out_weight: bfloat16 [2, 4096, 2048], P(None, None, ('dp', 'seq')), may hold values from -0.09375 to 0.09375
- cotangent: bfloat16 [2, 8192, 2048], P(None, ('dp', 'seq')), may hold values from -6 to 6
Outputs:
- block_out: bfloat16 [2, 8192, 2048], P(None, ('dp', 'seq'))
- grad_hidden: float32 [2, 8192, 2048], P(None, ('dp', 'seq'))
- grad_normgain: float32 [2, 2048], P(None, ('dp', 'seq'))
- grad_inproj: float32 [2, 2048, 8512], P(None, ('dp', 'seq'))
- grad_convtaps: float32 [2, 4, 4352], P(None, None, ('dp', 'seq'))
- grad_convbias: float32 [2, 4352], P(None, ('dp', 'seq'))
- grad_stepbias: float32 [2, 64], P(None, 'seq')
- grad_decay: float32 [2, 64], P(None, 'seq')
- grad_skip: float32 [2, 64], P(None, 'seq')
- grad_gategain: float32 [2, 4096], P(None, ('dp', 'seq'))
- grad_outproj: float32 [2, 4096, 2048], P(None, None, ('dp', 'seq'))
The draws below stay inside these ranges and needn't reach their ends.
Inputs may be any that keep to these rules, and one draw needn't show every extreme that they name: For each group and micro-batch the 3 lengths sum to 2048, and the longest has exactly 1024 tokens. `token_order`: for each group and micro-batch a permutation of the packed positions.
All inputs are finite; a program needn't handle non-finite values.
Results may differ from the reference program's by a relative error of at most 0.023.
Values may be sent and summed in bfloat16 or wider, within the bound.
No kernel may reach another device: no remote copies, remote signals or barrier semaphores. Data moves between devices by JAX's collectives and lax.ppermute only.
A program may use at most 512 MiB of HBM per device.

```python
import math
import jax
import jax.numpy as jnp
import numpy as np
from jax import lax

D = 2048
DI = 4096
H = 64
N = 128
CONV = 4
BLOCK = 256
LAYERS = 2
MB = 2
SEQS = 3
GROUP_TOK = 2048
TOKENS = 8192
XBC = 4352
PROJ = 8512
N_DP = 4


def draw_skip_gain(key, part):
    key = jax.random.fold_in(key, 7)
    places = jnp.arange(H, dtype=jnp.float32) / (H - 1)
    factor = jnp.exp(jax.random.uniform(key, (LAYERS, H), jnp.float32, -0.3, 0.3))
    result = 0.4 * jnp.power(3.0, places)[None, :] * factor
    return result.astype(jnp.float32)


def shard_levels(key, dims, shards, smallest, high):
    def one(dim, blocks):
        steps = jax.random.uniform(jax.random.fold_in(jax.random.fold_in(key, 6), dim), (blocks,), jnp.float32, smallest / len(shards), high / len(shards))
        return jnp.repeat(jnp.exp(steps), dims[dim] // blocks).reshape((-1,) + (1,) * (len(dims) - dim - 1))

    level = one(*shards[0])
    for cut in shards[1:]:
        level = level * one(*cut)
    return level


def split_up(count, total, reach, skew):
    portions = [(1 << 20) // math.isqrt(standing ** skew) + 1 for standing in range(2, count + 1)]
    rest, counts = total - reach - (count - 1), [1] * (count - 1)
    while rest > 0:
        movable = [i for i in range(count - 1) if counts[i] < reach]
        whole, remaining = sum([portions[i] for i in movable]), rest
        for i in movable:
            extra = min(reach - counts[i], max(1, remaining * portions[i] // whole), rest)
            counts[i] = counts[i] + extra
            rest = rest - extra
    return np.array([reach] + counts)


def ragged_sizes(rng, count, total, bound, slope):
    if count == 2:
        one = jax.random.randint(rng, (), max(1, total - bound), min(bound, total - 1) + 1)
        return jnp.stack([one, total - one])
    sizes = jnp.asarray(split_up(count, total, bound, slope), jnp.int32)
    couples = (count - 1) // 2
    donor, receiver = sizes[1:1 + 2 * couples:2], sizes[2:2 + 2 * couples:2]
    margin = jnp.minimum(donor - 1, bound - receiver)
    moved = jax.random.randint(jax.random.fold_in(rng, 1), (couples,), 0, 1 << 20) % (margin + 1)
    sizes = sizes.at[1:1 + 2 * couples:2].set(donor - moved).at[2:2 + 2 * couples:2].set(receiver + moved)
    return sizes[jax.random.permutation(jax.random.fold_in(rng, 2), count)]


def bell_draw(rng, shape, scale, bound, cuts=(), held_as=jnp.bfloat16):
    values = jax.random.normal(rng, shape, jnp.float32) * scale
    if len(cuts) > 0:
        values = shard_levels(rng, shape, cuts, -0.22, 0.18) * values
    return jnp.clip(values, min=-bound, max=bound).astype(held_as)


def setup_inputs(seed: int = 0) -> dict:
    keys = jax.random.split(jax.random.key(seed), 14)
    hidden = bell_draw(keys[0], (MB, TOKENS, D), 1.0, 6.0, ((1, 32),))
    lengths = jax.vmap(lambda own: ragged_sizes(own, SEQS, GROUP_TOK, GROUP_TOK // 2, 2))(jax.random.split(keys[1], MB * N_DP)).reshape((MB, N_DP, SEQS)).astype(jnp.int32)
    token_order = jax.vmap(lambda own: jax.random.permutation(own, GROUP_TOK))(jax.random.split(keys[2], MB * N_DP)).reshape((MB, N_DP, GROUP_TOK)).astype(jnp.int32)
    norm_gain = jnp.clip(1.0 + 0.18 * jax.random.normal(keys[3], (LAYERS, D), jnp.float32), 0.099609375, 1.8984375).astype(jnp.bfloat16)
    in_weight = bell_draw(keys[4], (LAYERS, D, PROJ), D ** -0.5, 0.125, ((1, 32),))
    conv_weight = jnp.clip(jax.random.uniform(keys[5], (LAYERS, CONV, XBC), jnp.float32, -0.5, 0.5) * shard_levels(keys[5], (LAYERS, CONV, XBC), ((2, 32),), -0.4, 0.0), -0.5, 0.5).astype(jnp.bfloat16)
    conv_bias = jnp.clip(jax.random.uniform(keys[6], (LAYERS, XBC), jnp.float32, -0.5, 0.5) * shard_levels(keys[6], (LAYERS, XBC), ((1, 32),), -0.4, 0.0), -0.5, 0.5).astype(jnp.bfloat16)
    dt_bias = jnp.clip(-4.0 + 3.0 * jax.random.uniform(keys[7], (LAYERS, H), jnp.float32) ** shard_levels(keys[7], (LAYERS, H), ((1, 8),), -0.2, 0.2), -4.0, -1.0)
    log_decay = jnp.clip(-4.0 + 6.5 * jax.random.uniform(keys[8], (LAYERS, H), jnp.float32) ** shard_levels(keys[8], (LAYERS, H), ((1, 8),), -0.2, 0.2), -4.0, 2.5)
    skip_gain = draw_skip_gain(jax.random.fold_in(keys[13], 71), 0)
    gate_gain = jnp.clip(1.0 + 0.18 * jax.random.normal(keys[10], (LAYERS, DI), jnp.float32), 0.099609375, 1.8984375).astype(jnp.bfloat16)
    out_weight = bell_draw(keys[11], (LAYERS, DI, D), DI ** -0.5, 0.09375, ((2, 32),))
    cotangent = bell_draw(keys[12], (MB, TOKENS, D), 1.0, 6.0, ((1, 32),))
    return dict(hidden=hidden, lengths=lengths, token_order=token_order, norm_gain=norm_gain, in_weight=in_weight, conv_weight=conv_weight, conv_bias=conv_bias, dt_bias=dt_bias, log_decay=log_decay, skip_gain=skip_gain, gate_gain=gate_gain, out_weight=out_weight, cotangent=cotangent)


HIGH = lax.Precision.HIGHEST
EPS = 1e-05

@jax.custom_vjp
def low(v):
    return lax.optimization_barrier(v.astype(jnp.bfloat16)).astype(jnp.float32)

@jax.custom_vjp
def low_back(v):
    return v

def low_keep(v):
    return (low(v), None)

def low_pass(kept, grad):
    return (grad,)

def back_keep(v):
    return (v, None)

def back_low(kept, grad):
    return (low(grad),)
low.defvjp(low_keep, low_pass)
low_back.defvjp(back_keep, back_low)

def segments_of(sizes, total):
    ends = jnp.cumsum(sizes).astype(jnp.int32)
    places = jnp.arange(total, dtype=jnp.int32)
    return lax.optimization_barrier(jnp.sum((places[:, None] >= ends[None, :]).astype(jnp.int32), axis=1)).astype(jnp.int32)

def inverse_of(perm):
    count = perm.shape[0]
    return jnp.zeros((count,), jnp.int32).at[perm].set(jnp.arange(count, dtype=jnp.int32))

def causal_conv(values, segs, taps, shift):
    width = taps.shape[0]
    total = values.shape[0]
    padded = jnp.concatenate([jnp.zeros((width - 1, values.shape[1]), values.dtype), values], axis=0)
    segpad = jnp.concatenate([jnp.full((width - 1,), -1, jnp.int32), segs.astype(jnp.int32)])
    result = jnp.zeros_like(values) + shift[None, :]
    for place in range(width):
        same = (segpad[place:place + total] == segs).astype(values.dtype)
        result = result + taps[place][None, :] * padded[place:place + total] * same[:, None]
    return result

def scan_blocks(inputs, steps, rates, bmat, cmat, segs, block):
    total, heads, size = inputs.shape
    states = bmat.shape[1]
    count = total // block
    places = jnp.arange(block, dtype=jnp.int32)
    lower = (places[:, None] >= places[None, :]).astype(inputs.dtype)

    def advance(carry, piece):
        state, before = carry
        xblock, sblock, bblock, cblock, gblock = piece
        logs = sblock * rates[None, :]
        cums = jnp.dot(lower, logs, precision=HIGH)
        same = ((gblock[:, None] == gblock[None, :]) & (lower > 0)).astype(inputs.dtype)
        diffs = cums[:, None, :] - cums[None, :, :]
        decays = jnp.exp(jnp.where(same[:, :, None] > 0, diffs, 0.0)) * same[:, :, None]
        scores = jnp.dot(cblock, bblock.T, precision=HIGH)
        weights = scores[:, :, None] * decays * sblock[None, :, :]
        inner = jnp.einsum('ijh,jhp->ihp', weights, xblock, precision=HIGH)
        keep = (gblock == before).astype(inputs.dtype)
        into = jnp.exp(cums) * keep[:, None]
        carried = jnp.einsum('in,hpn->ihp', cblock, state, precision=HIGH) * into[:, :, None]
        final = gblock[block - 1]
        tail = jnp.exp(cums[block - 1][None, :] - cums) * (gblock == final).astype(inputs.dtype)[:, None] * sblock
        fresh = jnp.einsum('jh,jhp,jn->hpn', tail, xblock, bblock, precision=HIGH)
        state = state * (jnp.exp(cums[block - 1]) * keep[block - 1])[:, None, None] + fresh
        return ((state, final), inner + carried)
    pieces = (inputs.reshape(count, block, heads, size), steps.reshape(count, block, heads), bmat.reshape(count, block, states), cmat.reshape(count, block, states), segs.reshape(count, block))
    start = (jnp.zeros((heads, size, states), inputs.dtype), jnp.array(-1, jnp.int32))
    finish, outputs = lax.scan(jax.checkpoint(advance), start, pieces)
    return outputs.reshape(total, heads, size)

def mixer_heads(xpart, bcraw, stepraw, taps_x, shift_x, taps_bc, shift_bc, step_bias, decay_log, skip, segs):
    total, width = xpart.shape
    heads = stepraw.shape[1]
    states = bcraw.shape[1] // 2
    acts = jax.nn.silu(causal_conv(xpart, segs, taps_x, shift_x))
    bcact = jax.nn.silu(causal_conv(bcraw, segs, taps_bc, shift_bc))
    steps = jax.nn.softplus(stepraw + step_bias[None, :])
    rates = -jnp.exp(decay_log)
    values = acts.reshape(total, heads, width // heads)
    mixed = scan_blocks(values, steps, rates, bcact[:, :states], bcact[:, states:], segs, BLOCK)
    mixed = mixed + skip[None, :, None] * values
    return mixed.reshape(total, width)

def pre_norm(rows, gain):
    return rows * lax.rsqrt(lax.optimization_barrier(jnp.mean(rows * rows, axis=1, keepdims=True)) + EPS) * gain[None, :]

def gate_norm(mixed, gatez, gain):
    gated = mixed * jax.nn.silu(gatez)
    return gated * lax.rsqrt(lax.optimization_barrier(jnp.mean(gated * gated, axis=1, keepdims=True)) + EPS) * gain[None, :]

def one_layer(rows, segs, params):
    ngain, win, taps, shift, sbias, dlog, skip, ggain, wout = params
    normed = low(pre_norm(rows, ngain))
    proj = low_back(low(jnp.dot(normed, win, precision=HIGH)))
    gatez = proj[:, :DI]
    xpart = proj[:, DI:2 * DI]
    bcraw = proj[:, 2 * DI:2 * DI + 2 * N]
    stepraw = proj[:, 2 * DI + 2 * N:]
    mixed = mixer_heads(xpart, bcraw, stepraw, taps[:, :DI], shift[:DI], taps[:, DI:], shift[DI:], sbias, dlog, skip, segs)
    mixed = low_back(low(mixed))
    normed2 = low(gate_norm(mixed, gatez, ggain))
    branch = low_back(jnp.dot(normed2, wout, precision=HIGH))
    return rows + branch

def reference(hidden, lengths, token_order, norm_gain, in_weight, conv_weight, conv_bias, dt_bias, log_decay, skip_gain, gate_gain, out_weight, cotangent):
    seg_all = jax.vmap(lambda sizes: segments_of(sizes, GROUP_TOK))(lengths.reshape(-1, SEQS))
    perm_all = token_order.reshape(-1, GROUP_TOK).astype(jnp.int32)
    inv_all = jax.vmap(inverse_of)(perm_all)
    params = (norm_gain.astype(jnp.float32), in_weight.astype(jnp.float32), conv_weight.astype(jnp.float32), conv_bias.astype(jnp.float32), dt_bias.astype(jnp.float32), log_decay.astype(jnp.float32), skip_gain.astype(jnp.float32), gate_gain.astype(jnp.float32), out_weight.astype(jnp.float32))

    def whole(rows_all, ngain, win, taps, shift, sbias, dlog, skip, ggain, wout):
        stacked = (ngain, win, taps, shift, sbias, dlog, skip, ggain, wout)
        flat = rows_all.reshape(MB * N_DP, GROUP_TOK, rows_all.shape[2])

        def group(item):
            rows, segs, perm, inv = item
            state = rows[inv]
            for layer in range(LAYERS):
                state = one_layer(state, segs, tuple((p[layer] for p in stacked)))
            return state[perm]
        result = lax.map(jax.checkpoint(group), (flat, seg_all, perm_all, inv_all))
        return result.reshape(rows_all.shape)
    result, pull = jax.vjp(whole, hidden.astype(jnp.float32), *params)
    grads = pull(cotangent.astype(jnp.float32))
    return (result.astype(jnp.bfloat16), grads[0], grads[1], grads[2], grads[3], grads[4], grads[5], grads[6], grads[7], grads[8], grads[9])
```

```python
import jax
import jax.numpy as jnp
from jax import lax
from jax.experimental import pallas as pl
from jax.experimental.pallas import tpu as pltpu
from jax.sharding import Mesh
from jax.sharding import PartitionSpec as P

DI = 4096
N = 128
CONV = 4
EPS = 1e-05
PARTS = 1
DEPTH = 4
SWAP = ((0, 1), (1, 0))
CHUNK = 256
LANES = 128
HEAD = 64
FAR = -1e30
VMEM_BYTES = 52 * 1024 * 1024


def sigmoid(v):
    return 0.5 * jnp.tanh(0.5 * v) + 0.5


def dot(a, b):
    return jnp.dot(a, b, preferred_element_type=jnp.float32)


def dot_nt(a, b):
    return lax.dot_general(a, b, (((1,), (1,)), ((), ())), preferred_element_type=jnp.float32)


def dot_tn(a, b):
    return lax.dot_general(a, b, (((0,), (0,)), ((), ())), preferred_element_type=jnp.float32)


def split3(v):
    hi = v.astype(jnp.bfloat16)
    rest = v - hi.astype(jnp.float32)
    mid = rest.astype(jnp.bfloat16)
    lo = (rest - mid.astype(jnp.float32)).astype(jnp.bfloat16)
    return hi, mid, lo


def pack3(v):
    hi, mid, lo = split3(v)
    lane = lax.broadcasted_iota(jnp.int32, v.shape, 1)
    mid = pltpu.roll(mid.astype(jnp.float32), 32, 1)
    lo = pltpu.roll(lo.astype(jnp.float32), 64, 1)
    joined = jnp.where(
        lane < 32, hi.astype(jnp.float32), jnp.where(lane < 64, mid, jnp.where(lane < 96, lo, 0.0))
    )
    return joined.astype(jnp.bfloat16)


def spread(rows_width, per):
    row = lax.broadcasted_iota(jnp.int32, (LANES, rows_width), 0)
    col = lax.broadcasted_iota(jnp.int32, (LANES, rows_width), 1)
    return ((row < 96) & (row % 32 == col // per)).astype(jnp.bfloat16)


def exact_left(matrix, v):
    hi, mid, lo = split3(v)
    return dot(matrix, hi) + dot(matrix, mid) + dot(matrix, lo)


def chunk_setup(st_ref, meta_ref, segrow_ref, hp_ref, chunk, cumb_ref, cumt_ref, mask_ref, wide_ref, tall_ref):
    raw = st_ref[...].astype(jnp.float32) + hp_ref[0:1, :]
    steps = jnp.maximum(raw, 0.0) + jnp.log1p(jnp.exp(-jnp.abs(raw)))
    row = lax.broadcasted_iota(jnp.int32, (chunk, chunk), 0)
    col = lax.broadcasted_iota(jnp.int32, (chunk, chunk), 1)
    lower = (row >= col).astype(jnp.bfloat16)
    cum = exact_left(lower, steps * hp_ref[1:2, :])
    cumb_ref[...] = dot(pack3(cum), tall_ref[...])
    cumt_ref[...] = cum.T
    seg = meta_ref[:, 5:6]
    same = jnp.broadcast_to(seg, (chunk, chunk)) == segrow_ref[0]
    mask_ref[...] = jnp.where(same & (row >= col), 0.0, FAR)
    e = jnp.exp(cum) * meta_ref[:, 3:4]
    decay = jnp.exp(cum[chunk - 1 : chunk, :] - cum) * meta_ref[:, 4:5]
    return raw, steps, cum, e, decay


def conv_parts(pad_ref, sl, chunk, cw, masks):
    here = pad_ref[8 : 8 + chunk, sl]
    back = [pad_ref[8 - m : 8 - m + chunk, sl] * masks[m - 1] for m in (1, 2, 3)]
    pre = cw[4:5, :] + cw[3:4, :] * here
    for m in (1, 2, 3):
        pre = pre + cw[3 - m : 4 - m, :] * back[m - 1]
    return pre, back, here


def forward_kernel(
    gate_ref, x_ref, bc_ref, st_ref, hx_ref, hbc_ref, meta_ref, segrow_ref, cw_ref, cbc_ref, hp_ref, s0_ref,
    mix_ref, gn_ref, ss_ref, states_ref, sout_ref,
    xpad, bpad, masks, cumb_ref, cumt_ref, mask_ref, sexp, eexp, texp, wide_ref, tall_ref, g_ref,
):
    chunk, width = x_ref.shape
    step = pl.program_id(0)

    @pl.when(step == 0)
    def _():
        sout_ref[...] = s0_ref[...]
        xpad[0:8, :] = hx_ref[8:16, :].astype(jnp.float32)
        bpad[0:8, :] = hbc_ref[8:16, :].astype(jnp.float32)
        wide_ref[...] = spread(width, HEAD)
        tall_ref[...] = spread(width * 2, LANES)

    @pl.when(step > 0)
    def _():
        xpad[0:8, :] = xpad[chunk : chunk + 8, :]
        bpad[0:8, :] = bpad[chunk : chunk + 8, :]

    xpad[8 : 8 + chunk, :] = x_ref[...].astype(jnp.float32)
    bpad[8 : 8 + chunk, :] = bc_ref[...].astype(jnp.float32)
    states_ref[0] = sout_ref[...]
    raw, steps, cum, e, decay = chunk_setup(
        st_ref, meta_ref, segrow_ref, hp_ref, chunk, cumb_ref, cumt_ref, mask_ref, wide_ref, tall_ref
    )
    for m in range(3):
        masks[m] = jnp.broadcast_to(meta_ref[:, m : m + 1], (chunk, LANES))
    sexp[...] = dot(pack3(steps), wide_ref[...])
    eexp[...] = dot(pack3(e), wide_ref[...])
    texp[...] = dot(pack3(decay * steps), wide_ref[...])
    bcact = []
    for half in range(2):
        sl = slice(half * LANES, (half + 1) * LANES)
        pre, _, _ = conv_parts(bpad, sl, chunk, cbc_ref[:, sl], masks)
        bcact.append((pre * sigmoid(pre)).astype(jnp.bfloat16))
    bmat, cmat = bcact
    g_ref[...] = dot_nt(cmat, bmat)
    low_lane = lax.broadcasted_iota(jnp.int32, (chunk, LANES), 1) < HEAD
    ss_ref[...] = jnp.zeros_like(ss_ref)

    def pair(p, carry):
        start = pl.multiple_of(p * LANES, LANES)
        sl = pl.ds(start, LANES)
        cw = cw_ref[:, sl]
        pre, _, _ = conv_parts(xpad, sl, chunk, cw, masks)
        xact = pre * sigmoid(pre)
        xs = (xact * sexp[:, sl]).astype(jnp.bfloat16)
        halves = []
        for k in range(2):
            h = 2 * p + k
            cumb = cumb_ref[:, pl.ds(pl.multiple_of(h * LANES, LANES), LANES)]
            cumb = jnp.concatenate([cumb] * (chunk // LANES), axis=1)
            decays = jnp.exp(cumb - cumt_ref[pl.ds(h, 1), :] + mask_ref[...])
            halves.append(dot((g_ref[...] * decays).astype(jnp.bfloat16), xs))
        inner = jnp.where(low_lane, halves[0], halves[1])
        state = sout_ref[:, sl]
        into = eexp[:, sl]
        carried = dot(cmat, state.astype(jnp.bfloat16)) * into
        fresh = dot_tn(bmat, (xact * texp[:, sl]).astype(jnp.bfloat16))
        sout_ref[:, sl] = state * into[chunk - 1 : chunk, :] + fresh
        mixbar = (inner + carried + cw[5:6, :] * xact).astype(jnp.bfloat16)
        mix_ref[:, sl] = mixbar
        gz = gate_ref[:, sl].astype(jnp.float32)
        gated = mixbar.astype(jnp.float32) * (gz * sigmoid(gz))
        gn_ref[:, sl] = (gated * cw[6:7, :]).astype(jnp.bfloat16)
        ss_ref[...] += gated * gated
        return carry

    lax.fori_loop(0, width // LANES, pair, 0)


def common_specs(chunk, width, order):
    bc_at, st_at = 2 * width // 256, (2 * width + 256) // LANES
    return [
        pl.BlockSpec((chunk, width), lambda c: (order(c), 0)),
        pl.BlockSpec((chunk, width), lambda c: (order(c), 1)),
        pl.BlockSpec((chunk, 256), lambda c: (order(c), bc_at)),
        pl.BlockSpec((chunk, LANES), lambda c: (order(c), st_at)),
    ]


def fixed(shape):
    return pl.BlockSpec(shape, lambda c: (0,) * len(shape))


def mixer_forward(proj, halo, meta, segrow, cw, cbc, hp, state, chunk=CHUNK):
    rows = proj.shape[0]
    width = cw.shape[1]
    count = rows // chunk
    same = lambda c: c
    bc_at = 2 * width // 256
    f32 = jnp.float32
    return pl.pallas_call(
        forward_kernel,
        grid=(count,),
        in_specs=common_specs(chunk, width, same)
        + [
            pl.BlockSpec((16, width), lambda c: (0, 1)),
            pl.BlockSpec((16, 256), lambda c: (0, bc_at)),
            pl.BlockSpec((chunk, 8), lambda c: (c, 0)),
            pl.BlockSpec((1, 1, chunk), lambda c: (c, 0, 0)),
            fixed((8, width)),
            fixed((8, 256)),
            fixed((8, LANES)),
            fixed((N, width)),
        ],
        out_specs=[
            pl.BlockSpec((chunk, width), lambda c: (c, 0)),
            pl.BlockSpec((chunk, width), lambda c: (c, 0)),
            pl.BlockSpec((chunk, LANES), lambda c: (c, 0)),
            pl.BlockSpec((1, N, width), lambda c: (c, 0, 0)),
            fixed((N, width)),
        ],
        out_shape=[
            jax.ShapeDtypeStruct((rows, width), jnp.bfloat16),
            jax.ShapeDtypeStruct((rows, width), jnp.bfloat16),
            jax.ShapeDtypeStruct((rows, LANES), f32),
            jax.ShapeDtypeStruct((count, N, width), f32),
            jax.ShapeDtypeStruct((N, width), f32),
        ],
        scratch_shapes=[
            pltpu.VMEM((chunk + 8, width), f32),
            pltpu.VMEM((chunk + 8, 256), f32),
            pltpu.VMEM((3, chunk, LANES), f32),
            pltpu.VMEM((chunk, 2 * width), f32),
            pltpu.VMEM((LANES, chunk), f32),
            pltpu.VMEM((chunk, chunk), f32),
            pltpu.VMEM((chunk, width), f32),
            pltpu.VMEM((chunk, width), f32),
            pltpu.VMEM((chunk, width), f32),
            pltpu.VMEM((LANES, width), jnp.bfloat16),
            pltpu.VMEM((LANES, 2 * width), jnp.bfloat16),
            pltpu.VMEM((chunk, chunk), f32),
        ],
        compiler_params=pltpu.CompilerParams(
            vmem_limit_bytes=VMEM_BYTES, dimension_semantics=("arbitrary",)
        ),
        cost_estimate=pl.CostEstimate(
            flops=rows * width * 1200, bytes_accessed=rows * width * 12, transcendentals=rows * width * 6
        ),
        name="mix_fwd",
    )(proj, proj, proj, proj, halo, halo, meta, segrow, cw, cbc, hp, state)


def conv_back(dpre, taps, masks, here, back, dpad, tail_ref, sl, chunk, acc_ref):
    acc_ref[4:5, sl] += jnp.sum(dpre, axis=0, keepdims=True)
    acc_ref[3:4, sl] += jnp.sum(dpre * here, axis=0, keepdims=True)
    grad = taps[3:4, :] * dpre
    for m in (1, 2, 3):
        acc_ref[3 - m : 4 - m, sl] += jnp.sum(dpre * back[m - 1], axis=0, keepdims=True)
        masked = dpre * masks[m - 1]
        dpad[m - 1, 0:chunk, :] = masked
        dpad[m - 1, chunk : chunk + 8, :] = tail_ref[m - 1, :, sl]
        tail_ref[m - 1, :, sl] = masked[0:8, :]
        grad = grad + taps[3 - m : 4 - m, :] * dpad[m - 1, m : m + chunk, :]
    return grad


def backward_kernel(
    gate_ref, x_ref, bc_ref, st_ref, px_ref, pbc_ref, hx_ref, hbc_ref, meta_ref, segrow_ref, cw_ref, cbc_ref, hp_ref,
    mix_ref, u_ref, fs_ref, states_ref, ds0_ref, tx0_ref, tbc0_ref,
    gproj_ref, n2_ref, acc_ref, accbc_ref, acch_ref, ds_ref, tx_ref, tbc_ref,
    xpad, bpad, masks, cumb_ref, cumt_ref, mask_ref, sexp, eexp, dexp, wide_ref, tall_ref, g_ref,
    dg_ref, db_ref, dc_ref, dcum_ref, dsx_ref, dpad, fac_ref, sb_ref,
):
    chunk, width = x_ref.shape
    step = pl.program_id(0)
    first = step == pl.num_programs(0) - 1

    @pl.when(step == 0)
    def _():
        ds_ref[...] = ds0_ref[...]
        tx_ref[...] = tx0_ref[...]
        tbc_ref[...] = tbc0_ref[...]
        acc_ref[...] = jnp.zeros_like(acc_ref)
        accbc_ref[...] = jnp.zeros_like(accbc_ref)
        acch_ref[...] = jnp.zeros_like(acch_ref)
        wide_ref[...] = spread(width, HEAD)
        tall_ref[...] = spread(width * 2, LANES)

    @pl.when(first)
    def _():
        xpad[0:8, :] = hx_ref[8:16, :].astype(jnp.float32)
        bpad[0:8, :] = hbc_ref[8:16, :].astype(jnp.float32)

    @pl.when(jnp.logical_not(first))
    def _():
        xpad[0:8, :] = px_ref[8:16, :].astype(jnp.float32)
        bpad[0:8, :] = pbc_ref[8:16, :].astype(jnp.float32)

    xpad[8 : 8 + chunk, :] = x_ref[...].astype(jnp.float32)
    bpad[8 : 8 + chunk, :] = bc_ref[...].astype(jnp.float32)
    raw, steps, cum, e, decay = chunk_setup(
        st_ref, meta_ref, segrow_ref, hp_ref, chunk, cumb_ref, cumt_ref, mask_ref, wide_ref, tall_ref
    )
    for m in range(3):
        masks[m] = jnp.broadcast_to(meta_ref[:, m : m + 1], (chunk, LANES))
    fac_ref[...] = jnp.broadcast_to(fs_ref[:, 0:1], (chunk, LANES))
    sb_ref[...] = jnp.broadcast_to(fs_ref[:, 1:2], (chunk, LANES))
    sexp[...] = dot(pack3(steps), wide_ref[...])
    eexp[...] = dot(pack3(e), wide_ref[...])
    dexp[...] = dot(pack3(decay), wide_ref[...])
    bcact, bcpre = [], []
    for half in range(2):
        sl = slice(half * LANES, (half + 1) * LANES)
        pre, back, here = conv_parts(bpad, sl, chunk, cbc_ref[:, sl], masks)
        bcact.append((pre * sigmoid(pre)).astype(jnp.bfloat16))
    bmat, cmat = bcact
    g_ref[...] = dot_nt(cmat, bmat)
    low_lane = lax.broadcasted_iota(jnp.int32, (chunk, LANES), 1) < HEAD
    last_row = lax.broadcasted_iota(jnp.int32, (chunk, LANES), 0) == chunk - 1
    dg_ref[...] = jnp.zeros_like(dg_ref)
    db_ref[...] = jnp.zeros_like(db_ref)
    dc_ref[...] = jnp.zeros_like(dc_ref)
    dcum_ref[...] = jnp.zeros_like(dcum_ref)
    dsx_ref[...] = jnp.zeros_like(dsx_ref)

    def pair(p, carry):
        start = pl.multiple_of(p * LANES, LANES)
        sl = pl.ds(start, LANES)
        cw = cw_ref[:, sl]
        gz = gate_ref[:, sl].astype(jnp.float32)
        sg = sigmoid(gz)
        active = gz * sg
        mixval = mix_ref[:, sl].astype(jnp.float32)
        gated = mixval * active
        fac = fac_ref[...]
        up = u_ref[:, sl].astype(jnp.float32) * fac
        dgated = up * cw[6:7, :] - gated * sb_ref[...]
        gm = (dgated * active).astype(jnp.bfloat16)
        gproj_ref[:, sl] = (dgated * mixval * sg * (1.0 + gz * (1.0 - sg))).astype(jnp.bfloat16)
        n2_ref[:, sl] = (gated * fac * cw[6:7, :]).astype(jnp.bfloat16)
        acc_ref[6:7, sl] += jnp.sum(gated * up, axis=0, keepdims=True)
        dy = gm.astype(jnp.float32)
        pre, back, here = conv_parts(xpad, sl, chunk, cw, masks)
        sig = sigmoid(pre)
        xact = pre * sig
        sx = sexp[:, sl]
        xs = (xact * sx).astype(jnp.bfloat16)
        xsf = xs.astype(jnp.float32)
        ys, dxs = [], []
        for k in range(2):
            h = 2 * p + k
            cumb = cumb_ref[:, pl.ds(pl.multiple_of(h * LANES, LANES), LANES)]
            cumb = jnp.concatenate([cumb] * (chunk // LANES), axis=1)
            decays = jnp.exp(cumb - cumt_ref[pl.ds(h, 1), :] + mask_ref[...])
            weights = (g_ref[...] * decays).astype(jnp.bfloat16)
            own = low_lane if k == 0 else jnp.logical_not(low_lane)
            pulls = dot_nt(jnp.where(own, dy, 0.0).astype(jnp.bfloat16), xs)
            dg_ref[...] += pulls * decays
            ys.append(dot(weights, xs))
            dxs.append(dot_tn(weights, gm))
        inner = jnp.where(low_lane, ys[0], ys[1])
        dinner = jnp.where(low_lane, dxs[0], dxs[1])
        state = states_ref[0, :, sl]
        stateb = state.astype(jnp.bfloat16)
        dstate = ds_ref[:, sl]
        dstateb = dstate.astype(jnp.bfloat16)
        into = eexp[:, sl]
        dec = dexp[:, sl]
        carried = dot(cmat, stateb) * into
        edy = (dy * into).astype(jnp.bfloat16)
        dc_ref[...] += dot_nt(edy, stateb)
        bds = dot(bmat, dstateb) * dec
        db_ref[...] += dot_nt((xsf * dec).astype(jnp.bfloat16), dstateb)
        tails = xsf * bds
        ends = jnp.sum(tails, axis=0, keepdims=True) + into[chunk - 1 : chunk, :] * jnp.sum(
            dstate * state, axis=0, keepdims=True
        )
        rowq = dy * (inner + carried) - xsf * dinner - tails + jnp.where(last_row, ends, 0.0)
        dxsum = dinner + bds
        row = lax.broadcasted_iota(jnp.int32, (LANES, LANES), 0)
        col = lax.broadcasted_iota(jnp.int32, (LANES, LANES), 1)
        gather = (col == 2 * p + row // HEAD).astype(jnp.bfloat16)
        hi, mid, lo = split3(rowq)
        dcum_ref[...] += dot(hi, gather) + dot(mid, gather) + dot(lo, gather)
        hi, mid, lo = split3(xact * dxsum)
        dsx_ref[...] += dot(hi, gather) + dot(mid, gather)
        ds_ref[:, sl] = dstate * into[chunk - 1 : chunk, :] + dot_tn(cmat, edy)
        acc_ref[5:6, sl] += jnp.sum(dy * xact, axis=0, keepdims=True)
        dact = sx * dxsum + cw[5:6, :] * dy
        dpre = dact * (sig * (1.0 + pre * (1.0 - sig)))
        grad = conv_back(dpre, cw, masks, here, back, dpad, tx_ref, sl, chunk, acc_ref)
        gproj_ref[:, pl.ds(pl.multiple_of(width + start, LANES), LANES)] = grad.astype(jnp.bfloat16)
        return carry

    lax.fori_loop(0, width // LANES, pair, 0)
    dgb = dg_ref[...].astype(jnp.bfloat16)
    grads = (db_ref[...] + dot_tn(dgb, cmat), dc_ref[...] + dot(dgb, bmat))
    for half in range(2):
        sl = slice(half * LANES, (half + 1) * LANES)
        cw = cbc_ref[:, sl]
        pre, back, here = conv_parts(bpad, sl, chunk, cw, masks)
        sig = sigmoid(pre)
        dpre = grads[half] * (sig * (1.0 + pre * (1.0 - sig)))
        grad = conv_back(dpre, cw, masks, here, back, dpad, tbc_ref, sl, chunk, accbc_ref)
        at = 2 * width + half * LANES
        gproj_ref[:, at : at + LANES] = grad.astype(jnp.bfloat16)
    row = lax.broadcasted_iota(jnp.int32, (chunk, chunk), 0)
    col = lax.broadcasted_iota(jnp.int32, (chunk, chunk), 1)
    upper = (col >= row).astype(jnp.bfloat16)
    dlogs = exact_left(upper, dcum_ref[...])
    dsteps = dsx_ref[...] + dlogs * hp_ref[1:2, :]
    draw = dsteps * sigmoid(raw)
    gproj_ref[:, 2 * width + 256 :] = draw.astype(jnp.bfloat16)
    acch_ref[0:1, :] += jnp.sum(draw, axis=0, keepdims=True)
    acch_ref[1:2, :] += jnp.sum(dlogs * steps, axis=0, keepdims=True)


def mixer_backward(proj, halo, meta, segrow, cw, cbc, hp, mix, up, fs, states, dstate, tx, tbc, chunk=CHUNK):
    rows, cols = proj.shape
    width = cw.shape[1]
    count = rows // chunk
    back = lambda c: count - 1 - c
    bc_at = 2 * width // 256
    f32 = jnp.float32
    per = chunk // 16
    before = lambda c: jnp.maximum(back(c) * per - 1, 0)
    return pl.pallas_call(
        backward_kernel,
        grid=(count,),
        in_specs=common_specs(chunk, width, back)
        + [
            pl.BlockSpec((16, width), lambda c: (before(c), 1)),
            pl.BlockSpec((16, 256), lambda c: (before(c), bc_at)),
            pl.BlockSpec((16, width), lambda c: (0, 1)),
            pl.BlockSpec((16, 256), lambda c: (0, bc_at)),
            pl.BlockSpec((chunk, 8), lambda c: (back(c), 0)),
            pl.BlockSpec((1, 1, chunk), lambda c: (back(c), 0, 0)),
            fixed((8, width)),
            fixed((8, 256)),
            fixed((8, LANES)),
            pl.BlockSpec((chunk, width), lambda c: (back(c), 0)),
            pl.BlockSpec((chunk, width), lambda c: (back(c), 0)),
            pl.BlockSpec((chunk, 8), lambda c: (back(c), 0)),
            pl.BlockSpec((1, N, width), lambda c: (back(c), 0, 0)),
            fixed((N, width)),
            fixed((3, 8, width)),
            fixed((3, 8, 256)),
        ],
        out_specs=[
            pl.BlockSpec((chunk, cols), lambda c: (back(c), 0)),
            pl.BlockSpec((chunk, width), lambda c: (back(c), 0)),
            fixed((8, width)),
            fixed((8, 256)),
            fixed((8, LANES)),
            fixed((N, width)),
            fixed((3, 8, width)),
            fixed((3, 8, 256)),
        ],
        out_shape=[
            jax.ShapeDtypeStruct((rows, cols), jnp.bfloat16),
            jax.ShapeDtypeStruct((rows, width), jnp.bfloat16),
            jax.ShapeDtypeStruct((8, width), f32),
            jax.ShapeDtypeStruct((8, 256), f32),
            jax.ShapeDtypeStruct((8, LANES), f32),
            jax.ShapeDtypeStruct((N, width), f32),
            jax.ShapeDtypeStruct((3, 8, width), f32),
            jax.ShapeDtypeStruct((3, 8, 256), f32),
        ],
        scratch_shapes=[
            pltpu.VMEM((chunk + 8, width), f32),
            pltpu.VMEM((chunk + 8, 256), f32),
            pltpu.VMEM((3, chunk, LANES), f32),
            pltpu.VMEM((chunk, 2 * width), f32),
            pltpu.VMEM((LANES, chunk), f32),
            pltpu.VMEM((chunk, chunk), f32),
            pltpu.VMEM((chunk, width), f32),
            pltpu.VMEM((chunk, width), f32),
            pltpu.VMEM((chunk, width), f32),
            pltpu.VMEM((LANES, width), jnp.bfloat16),
            pltpu.VMEM((LANES, 2 * width), jnp.bfloat16),
            pltpu.VMEM((chunk, chunk), f32),
            pltpu.VMEM((chunk, chunk), f32),
            pltpu.VMEM((chunk, N), f32),
            pltpu.VMEM((chunk, N), f32),
            pltpu.VMEM((chunk, LANES), f32),
            pltpu.VMEM((chunk, LANES), f32),
            pltpu.VMEM((3, chunk + 8, LANES), f32),
            pltpu.VMEM((chunk, LANES), f32),
            pltpu.VMEM((chunk, LANES), f32),
        ],
        compiler_params=pltpu.CompilerParams(
            vmem_limit_bytes=VMEM_BYTES, dimension_semantics=("arbitrary",)
        ),
        cost_estimate=pl.CostEstimate(
            flops=rows * width * 4000, bytes_accessed=rows * width * 24, transcendentals=rows * width * 8
        ),
        name="mix_bwd",
    )(
        proj, proj, proj, proj, proj, proj, halo, halo, meta, segrow, cw, cbc, hp,
        mix, up, fs, states, dstate, tx, tbc,
    )


def token_facts(seg, chunk=CHUNK):
    total = seg.shape[0]
    place = jnp.arange(total, dtype=jnp.int32)
    cols = []
    for m in (1, 2, 3):
        before = jnp.concatenate([jnp.full((m,), -1, jnp.int32), seg[:-m]])
        cols.append(before == seg)
    ends = seg.reshape(-1, chunk)[:, -1]
    starts = jnp.concatenate([jnp.full((1,), -1, jnp.int32), ends[:-1]])
    cols.append(jnp.repeat(starts, chunk) == seg)
    cols.append(jnp.repeat(ends, chunk) == seg)
    meta = jnp.stack([c.astype(jnp.float32) for c in cols] + [seg.astype(jnp.float32)], axis=1)
    meta = jnp.pad(meta, ((0, 0), (0, 2)))
    return meta, seg.astype(jnp.float32).reshape(-1, 1, chunk)


def team_sizes():
    return lax.axis_size("x"), 2 * lax.axis_size("x")


def in_order(first, mine, theirs):
    return jnp.stack([jnp.where(first, mine, theirs), jnp.where(first, theirs, mine)])


def team_gather(own):
    across = lax.axis_size("x")
    if across == 2:
        row = in_order(lax.axis_index("x") == 0, own, lax.ppermute(own, "x", SWAP))
    else:
        row = lax.all_gather(own, "x", axis=0)
    both = in_order(lax.axis_index("core") == 0, row, lax.ppermute(row, "core", SWAP))
    return both.reshape((2 * across,) + own.shape)


def team_reduce(parts, kind):
    across = lax.axis_size("x")
    core = lax.axis_index("core")
    halves = parts.reshape((2, across) + parts.shape[1:])
    keep = lax.dynamic_index_in_dim(halves, core, 0, False)
    got = lax.ppermute(lax.dynamic_index_in_dim(halves, 1 - core, 0, False), "core", SWAP)
    if across == 2:
        place = lax.axis_index("x")

        def added(at):
            return lax.dynamic_index_in_dim(keep, at, 0, False).astype(jnp.float32) + (
                lax.dynamic_index_in_dim(got, at, 0, False).astype(jnp.float32)
            )

        far = lax.ppermute(added(1 - place).astype(kind), "x", SWAP)
        return added(place) + far.astype(jnp.float32)
    sums = (keep.astype(jnp.float32) + got.astype(jnp.float32)).astype(kind)
    return lax.psum_scatter(sums, "x", scatter_dimension=0, tiled=False).astype(jnp.float32)


def deal_moves():
    moves = []
    for r in range(2):
        pairs = []
        for core in range(2):
            for z in range(DEPTH):
                pairs.append((core * DEPTH + z, (z // 2) * DEPTH + 2 * core + ((z % 2) ^ r)))
        moves.append(pairs)
    return moves


def to_team(rows):
    low = lax.axis_index("z") % 2
    got = []
    for r, pairs in enumerate(deal_moves()):
        block = lax.dynamic_index_in_dim(rows, low ^ r, 0, False)
        got.append(lax.ppermute(block, ("core", "z"), pairs))
    return in_order(low == 0, got[0], got[1]).reshape(-1, rows.shape[2])


def from_team(rows):
    low = lax.axis_index("z") % 2
    blocks = rows.reshape(2, -1, rows.shape[1])
    got = []
    for r, pairs in enumerate(deal_moves()):
        block = lax.dynamic_index_in_dim(blocks, low ^ r, 0, False)
        got.append(lax.ppermute(block, ("core", "z"), [(b, a) for a, b in pairs]))
    return in_order(low == 0, got[0], got[1])


def inverse_of(perm):
    count = perm.shape[0]
    places = jnp.arange(count, dtype=jnp.int32)
    return jnp.sum(jnp.where(places[:, None] == perm[None, :], places[None, :], 0), axis=1)


def segments_of(sizes, total):
    ends = jnp.cumsum(sizes)
    places = jnp.arange(total, dtype=jnp.int32)
    return jnp.sum((places[:, None] >= ends[None, :]).astype(jnp.int32), axis=1)


def natural_rows(gathered):
    total, cols = gathered.shape
    view = gathered.reshape(lax.axis_size("y"), DEPTH, 2, -1, cols)
    return view.transpose(0, 2, 1, 3, 4).reshape(total, cols)


def plane_rows(natural):
    total, cols = natural.shape
    view = natural.reshape(lax.axis_size("y"), 2, DEPTH, -1, cols)
    return view.transpose(0, 2, 1, 3, 4).reshape(total, cols)


def to_heads(pieces):
    sent = lax.all_to_all(pieces, ("core", "x"), split_axis=1, concat_axis=0, tiled=True)
    sent = sent.reshape(-1, pieces.shape[2])
    return natural_rows(lax.all_gather(sent, ("y", "z"), axis=0, tiled=True))


def from_heads(grads):
    cols = grads.shape[1]
    team = 2 * lax.axis_size("x")
    summed = lax.psum_scatter(plane_rows(grads), ("y", "z"), scatter_dimension=0, tiled=True)
    back = lax.all_to_all(
        summed.reshape(team, -1, cols), ("core", "x"), split_axis=0, concat_axis=0, tiled=True
    )
    return back.transpose(1, 0, 2)


def in_columns(w_in, team):
    rows = w_in.shape[0]
    bc = w_in[:, 2 * DI : 2 * DI + 2 * N]
    step = w_in[:, 2 * DI + 2 * N :].reshape(rows, team, -1)
    return jnp.concatenate(
        [
            w_in[:, :DI].reshape(rows, team, -1),
            w_in[:, DI : 2 * DI].reshape(rows, team, -1),
            jnp.broadcast_to(bc[:, None, :], (rows, team, 2 * N)),
            step,
            jnp.zeros((rows, team, LANES - step.shape[2]), w_in.dtype),
        ],
        axis=2,
    )


def row_scale(rows):
    return lax.rsqrt(jnp.mean(rows * rows, axis=1, keepdims=True) + EPS)


def per_device(
    hidden,
    lengths,
    token_order,
    norm_gain,
    in_weight,
    conv_weight,
    conv_bias,
    dt_bias,
    log_decay,
    skip_gain,
    gate_gain,
    out_weight,
    cotangent,
):
    bf16, f32 = jnp.bfloat16, jnp.float32
    layers = in_weight.shape[0]
    across, team = team_sizes()
    core, z, x = (lax.axis_index(name) for name in ("core", "z", "x"))
    member = core * across + x
    width = DI // team
    heads = width // HEAD
    rows_here = hidden.shape[1]
    tokens = token_order.shape[2]
    part_rows = tokens // PARTS
    own_rows = part_rows // team

    def of_pair(ints):
        other = lax.ppermute(ints, "core", SWAP)
        return lax.dynamic_index_in_dim(jnp.where(z // 2 == core, ints, other), z % 2, 0, False)[0]

    order, sizes = of_pair(token_order), of_pair(lengths)
    inverse = inverse_of(order)
    block, within = inverse // rows_here, inverse % rows_here
    from_z, from_x = block // across, block % across
    place = ((from_z // 2 * across + from_x) * 2 + from_z % 2) * rows_here + within
    own_block = (2 * core + jnp.arange(2, dtype=jnp.int32)) * across + x
    own_dealt = (own_block[:, None] * rows_here + jnp.arange(rows_here, dtype=jnp.int32)).reshape(-1)
    meta, segrow = token_facts(segments_of(sizes, tokens))

    w_cols = [to_heads(in_columns(in_weight[layer], team)) for layer in range(layers)]
    w_out = [
        to_heads(out_weight[layer].T.reshape(-1, team, width)) for layer in range(layers)
    ]
    flat = jnp.concatenate(
        [conv_weight.reshape(layers, -1), conv_bias, norm_gain, gate_gain], axis=1
    )
    wide = conv_bias.shape[1]
    full = lax.all_gather(flat, ("y", "core", "z", "x"), axis=0).transpose(1, 0, 2)
    cuts = [CONV * wide, (CONV + 1) * wide, (CONV + 1) * wide + norm_gain.shape[1]]
    taps, shift, ngain, ggain = jnp.split(full.astype(f32), cuts, axis=2)
    taps = taps.reshape(layers, -1, CONV, wide).transpose(0, 2, 1, 3).reshape(layers, CONV, -1)
    shift, ngain, ggain = (v.reshape(layers, -1) for v in (shift, ngain, ggain))
    per_head = lax.all_gather(
        jnp.stack([dt_bias, log_decay, skip_gain]), ("z", "x"), axis=2, tiled=True
    )
    own_heads = lax.dynamic_slice_in_dim(per_head, member * heads, heads, 2)

    def mine(values):
        return lax.dynamic_slice_in_dim(values, member * width, width, values.ndim - 1)

    tables = []
    for layer in range(layers):
        cw = jnp.concatenate(
            [
                mine(taps[layer, :, :DI]),
                mine(shift[layer, None, :DI]),
                jnp.repeat(own_heads[2, layer], HEAD)[None],
                mine(ggain[layer, None]),
                jnp.zeros((1, width), f32),
            ]
        )
        cbc = jnp.concatenate(
            [taps[layer, :, DI:], shift[layer, None, DI:], jnp.zeros((3, 2 * N), f32)]
        )
        hp = jnp.stack([own_heads[0, layer], -jnp.exp(own_heads[1, layer])])
        tables.append((cw, cbc, jnp.pad(hp, ((0, 6), (0, LANES - heads)))))

    def packed(rows):
        gathered = team_gather(to_team(rows)).reshape(tokens, -1)
        return gathered[place]

    def part(values, i):
        return values[i * part_rows : (i + 1) * part_rows]

    def own_of(values):
        return lax.dynamic_slice_in_dim(values, member * own_rows, own_rows, 0)

    def facts(i):
        count = part_rows // CHUNK
        return part(meta, i), segrow[i * count : (i + 1) * count]

    everything = packed(hidden)
    states = [own_of(part(everything, i)).astype(f32) for i in range(PARTS)]
    record = []
    no_halo = jnp.zeros((16, 2 * width + 2 * N + LANES), bf16)
    for layer in range(layers):
        kept = []
        state = jnp.zeros((N, width), f32)
        halo = no_halo
        for i in range(PARTS):
            rows = states[i]
            if layer == 0:
                every = part(everything, i).astype(f32)
                normed = (every * row_scale(every) * ngain[layer]).astype(bf16)
            else:
                normed = (rows * row_scale(rows) * ngain[layer]).astype(bf16)
                normed = team_gather(normed).reshape(part_rows, -1)
            proj = jnp.dot(normed, w_cols[layer], preferred_element_type=f32).astype(bf16)
            mix, gated, squares, starts, state = mixer_forward(
                proj, halo, *facts(i), *tables[layer], state
            )
            partial = dot_nt(gated, w_out[layer]).astype(bf16)
            branch = team_reduce(partial.reshape(team, own_rows, -1), bf16)
            total = team_reduce(jnp.sum(squares, axis=1).reshape(team, own_rows), f32)
            factor = lax.rsqrt(total / DI + EPS)
            states[i] = rows + branch * factor[:, None]
            kept.append((rows, normed, proj, halo, mix, starts, branch.astype(bf16), factor))
            halo = proj[part_rows - 16 :]
        record.append(kept)

    def dealt(parts):
        whole = [team_gather(p.astype(bf16)).reshape(part_rows, -1) for p in parts]
        whole = jnp.concatenate(whole) if PARTS > 1 else whole[0]
        return from_team(whole[order[own_dealt]])

    block_out = dealt(states)
    gout_whole = packed(cotangent)
    grads_rows = [own_of(part(gout_whole, i)).astype(f32) for i in range(PARTS)]
    results = [None] * layers
    small = [None] * layers
    for layer in reversed(range(layers)):
        dstate = jnp.zeros((N, width), f32)
        tail_x = jnp.zeros((3, 8, width), f32)
        tail_bc = jnp.zeros((3, 8, 2 * N), f32)
        gathered, sums = [None] * PARTS, None
        for i in reversed(range(PARTS)):
            rows, normed, proj, halo, mix, starts, branch, factor = record[layer][i]
            gout = grads_rows[i].astype(bf16)
            inner = jnp.sum(gout.astype(f32) * branch.astype(f32), axis=1)
            scales = jnp.stack([factor, factor * factor * factor * inner / DI])
            scales = team_gather(scales).transpose(0, 2, 1).reshape(part_rows, 2)
            if layer == layers - 1:
                gout_all = part(gout_whole, i)
            else:
                gout_all = team_gather(gout).reshape(part_rows, -1)
            up = jnp.dot(gout_all, w_out[layer], preferred_element_type=f32).astype(bf16)
            gproj, normed2, acc, acc_bc, acc_h, dstate, tail_x, tail_bc = mixer_backward(
                proj,
                halo,
                *facts(i),
                *tables[layer],
                mix,
                up,
                jnp.pad(scales, ((0, 0), (0, 6))),
                starts,
                dstate,
                tail_x,
                tail_bc,
            )
            partial = dot_nt(gproj, w_cols[layer]).astype(bf16)
            gnormed = team_reduce(partial.reshape(team, own_rows, -1), bf16)
            scale = row_scale(rows)
            pulled = gnormed * ngain[layer]
            back = jnp.mean(pulled * rows, axis=1, keepdims=True)
            grads_rows[i] = grads_rows[i] + scale * pulled - rows * (scale * scale * scale * back)
            gathered[i] = (normed, gproj, gout_all, normed2)
            found = (acc, acc_bc, acc_h)
            sums = found if sums is None else tuple(a + b for a, b in zip(sums, found))
        if PARTS > 1:
            whole = [jnp.concatenate([g[k] for g in gathered]) for k in range(4)]
        else:
            whole = gathered[0]
        grad_out = from_heads(dot_tn(whole[2], whole[3]).astype(bf16))
        split = from_heads(dot_tn(whole[0], whole[1]).astype(bf16)).astype(f32)
        count = split.shape[0]
        bc_at = 2 * width
        step_at = bc_at + 2 * N
        grad_in = jnp.concatenate(
            [
                split[:, :, :width].reshape(count, DI),
                split[:, :, width:bc_at].reshape(count, DI),
                jnp.sum(split[:, :, bc_at:step_at], axis=1),
                split[:, :, step_at : step_at + heads].reshape(count, team * heads),
            ],
            axis=1,
        )
        grad_norm = jnp.sum(grad_in * in_weight[layer].astype(f32), axis=1) / (
            norm_gain[layer].astype(f32)
        )
        results[layer] = (grad_norm, grad_in, grad_out.astype(f32).reshape(count, DI).T)
        acc, acc_bc, acc_h = sums
        taps_full = jnp.zeros((CONV + 1, DI + 2 * N), f32)
        taps_full = lax.dynamic_update_slice(taps_full, acc[: CONV + 1], (0, member * width))
        taps_full = lax.dynamic_update_slice(taps_full, acc_bc[: CONV + 1], (0, DI))
        gate_full = lax.dynamic_update_slice(jnp.zeros((DI,), f32), acc[6], (member * width,))
        spread_out = jnp.concatenate(
            [
                taps_full.reshape(CONV + 1, -1, wide).transpose(1, 0, 2).reshape(-1, (CONV + 1) * wide),
                gate_full.reshape(-1, gate_gain.shape[1]),
            ],
            axis=1,
        )
        head_sums = jnp.stack(
            [
                acc_h[0, :heads],
                acc_h[1, :heads] * tables[layer][2][1, :heads],
                jnp.sum(acc[5].reshape(heads, HEAD), axis=1),
            ]
        )
        head_full = lax.dynamic_update_slice(
            jnp.zeros((3, team * heads), f32), head_sums, (0, member * heads)
        )
        small[layer] = (spread_out, head_full)
    grad_hidden = dealt(grads_rows).astype(f32)
    every_axis = ("y", "core", "z", "x")
    spread_sum = lax.psum_scatter(
        jnp.stack([s[0] for s in small], axis=1), every_axis, scatter_dimension=0, tiled=False
    )
    head_sum = lax.psum(jnp.stack([s[1] for s in small]), every_axis)
    here = dt_bias.shape[1]
    head_own = lax.dynamic_slice_in_dim(head_sum, (z * across + x) * here, here, 2)
    grad_taps = spread_sum[:, : CONV * wide].reshape(layers, CONV, wide)
    return (
        block_out,
        grad_hidden,
        jnp.stack([r[0] for r in results]),
        jnp.stack([r[1] for r in results]),
        grad_taps,
        spread_sum[:, CONV * wide : (CONV + 1) * wide],
        head_own[:, 0],
        head_own[:, 1],
        head_own[:, 2],
        spread_sum[:, (CONV + 1) * wide :],
        jnp.stack([r[2] for r in results]),
    )


def solution(mesh):
    grid = mesh.devices.reshape(mesh.shape["dp"] // 2, 2, DEPTH, mesh.shape["seq"] // DEPTH)
    fine = Mesh(grid, ("y", "core", "z", "x"))
    dp, seq = ("y", "core"), ("z", "x")
    both = dp + seq
    return jax.shard_map(
        per_device,
        mesh=fine,
        in_specs=(
            P(None, both, None),
            P(None, dp, None),
            P(None, dp, None),
            P(None, both),
            P(None, both, None),
            P(None, None, both),
            P(None, both),
            P(None, seq),
            P(None, seq),
            P(None, seq),
            P(None, both),
            P(None, None, both),
            P(None, both, None),
        ),
        out_specs=(
            P(None, both, None),
            P(None, both, None),
            P(None, both),
            P(None, both, None),
            P(None, None, both),
            P(None, both),
            P(None, seq),
            P(None, seq),
            P(None, seq),
            P(None, both),
            P(None, None, both),
        ),
        check_vma=False,
    )
```

```python
import jax
import jax.numpy as jnp
from jax import lax
from jax.experimental import pallas as pl
from jax.experimental.pallas import tpu as pltpu
from jax.sharding import Mesh
from jax.sharding import PartitionSpec as P

DI = 4096
N = 128
CONV = 4
EPS = 1e-05
PARTS = 2
DEPTH = 4
SWAP = ((0, 1), (1, 0))
CHUNK = 256
LANES = 128
HEAD = 64
FAR = -1e30
VMEM_BYTES = 52 * 1024 * 1024


def sigmoid(v):
    return 0.5 * jnp.tanh(0.5 * v) + 0.5


def dot(a, b):
    return jnp.dot(a, b, preferred_element_type=jnp.float32)


def dot_nt(a, b):
    return lax.dot_general(a, b, (((1,), (1,)), ((), ())), preferred_element_type=jnp.float32)


def dot_tn(a, b):
    return lax.dot_general(a, b, (((0,), (0,)), ((), ())), preferred_element_type=jnp.float32)


def split3(v):
    hi = v.astype(jnp.bfloat16)
    rest = v - hi.astype(jnp.float32)
    mid = rest.astype(jnp.bfloat16)
    lo = (rest - mid.astype(jnp.float32)).astype(jnp.bfloat16)
    return hi, mid, lo


def pack3(v):
    hi, mid, lo = split3(v)
    lane = lax.broadcasted_iota(jnp.int32, v.shape, 1)
    mid = pltpu.roll(mid.astype(jnp.float32), 32, 1)
    lo = pltpu.roll(lo.astype(jnp.float32), 64, 1)
    joined = jnp.where(
        lane < 32, hi.astype(jnp.float32), jnp.where(lane < 64, mid, jnp.where(lane < 96, lo, 0.0))
    )
    return joined.astype(jnp.bfloat16)


def spread(rows_width, per):
    row = lax.broadcasted_iota(jnp.int32, (LANES, rows_width), 0)
    col = lax.broadcasted_iota(jnp.int32, (LANES, rows_width), 1)
    return ((row < 96) & (row % 32 == col // per)).astype(jnp.bfloat16)


def exact_left(matrix, v):
    hi, mid, lo = split3(v)
    return dot(matrix, hi) + dot(matrix, mid) + dot(matrix, lo)


def chunk_setup(st_ref, meta_ref, segrow_ref, hp_ref, chunk, cumb_ref, cumt_ref, mask_ref, wide_ref, tall_ref):
    raw = st_ref[...].astype(jnp.float32) + hp_ref[0:1, :]
    steps = jnp.maximum(raw, 0.0) + jnp.log1p(jnp.exp(-jnp.abs(raw)))
    row = lax.broadcasted_iota(jnp.int32, (chunk, chunk), 0)
    col = lax.broadcasted_iota(jnp.int32, (chunk, chunk), 1)
    lower = (row >= col).astype(jnp.bfloat16)
    cum = exact_left(lower, steps * hp_ref[1:2, :])
    cumb_ref[...] = dot(pack3(cum), tall_ref[...])
    cumt_ref[...] = cum.T
    seg = meta_ref[:, 5:6]
    same = jnp.broadcast_to(seg, (chunk, chunk)) == segrow_ref[0]
    mask_ref[...] = jnp.where(same & (row >= col), 0.0, FAR)
    e = jnp.exp(cum) * meta_ref[:, 3:4]
    decay = jnp.exp(cum[chunk - 1 : chunk, :] - cum) * meta_ref[:, 4:5]
    return raw, steps, cum, e, decay


def conv_parts(pad_ref, sl, chunk, cw, masks):
    here = pad_ref[8 : 8 + chunk, sl]
    back = [pad_ref[8 - m : 8 - m + chunk, sl] * masks[m - 1] for m in (1, 2, 3)]
    pre = cw[4:5, :] + cw[3:4, :] * here
    for m in (1, 2, 3):
        pre = pre + cw[3 - m : 4 - m, :] * back[m - 1]
    return pre, back, here


def forward_kernel(
    perm_ref, gate_ref, x_ref, bc_ref, st_ref, hx_ref, hbc_ref, meta_ref, segrow_ref, cw_ref, cbc_ref, hp_ref, s0_ref,
    mix_ref, gn_ref, ss_ref, states_ref, sout_ref,
    xpad, bpad, masks, cumb_ref, cumt_ref, mask_ref, sexp, eexp, texp, wide_ref, tall_ref, g_ref,
):
    chunk, width = x_ref.shape
    step = pl.program_id(0)

    @pl.when(step == 0)
    def _():
        sout_ref[...] = s0_ref[...]
        xpad[0:8, :] = hx_ref[8:16, :].astype(jnp.float32)
        bpad[0:8, :] = hbc_ref[8:16, :].astype(jnp.float32)
        wide_ref[...] = spread(width, HEAD)
        tall_ref[...] = spread(width * 2, LANES)

    @pl.when(step > 0)
    def _():
        xpad[0:8, :] = xpad[chunk : chunk + 8, :]
        bpad[0:8, :] = bpad[chunk : chunk + 8, :]

    xpad[8 : 8 + chunk, :] = x_ref[...].astype(jnp.float32)
    bpad[8 : 8 + chunk, :] = bc_ref[...].astype(jnp.float32)
    states_ref[0] = sout_ref[...]
    raw, steps, cum, e, decay = chunk_setup(
        st_ref, meta_ref, segrow_ref, hp_ref, chunk, cumb_ref, cumt_ref, mask_ref, wide_ref, tall_ref
    )
    for m in range(3):
        masks[m] = jnp.broadcast_to(meta_ref[:, m : m + 1], (chunk, LANES))
    sexp[...] = dot(pack3(steps), wide_ref[...])
    eexp[...] = dot(pack3(e), wide_ref[...])
    texp[...] = dot(pack3(decay * steps), wide_ref[...])
    bcact = []
    for half in range(2):
        sl = slice(half * LANES, (half + 1) * LANES)
        pre, _, _ = conv_parts(bpad, sl, chunk, cbc_ref[:, sl], masks)
        bcact.append((pre * sigmoid(pre)).astype(jnp.bfloat16))
    bmat, cmat = bcact
    g_ref[...] = dot_nt(cmat, bmat)
    low_lane = lax.broadcasted_iota(jnp.int32, (chunk, LANES), 1) < HEAD
    ss_ref[...] = jnp.zeros_like(ss_ref)

    def pair(p, carry):
        start = pl.multiple_of(p * LANES, LANES)
        sl = pl.ds(start, LANES)
        cw = cw_ref[:, sl]
        pre, _, _ = conv_parts(xpad, sl, chunk, cw, masks)
        xact = pre * sigmoid(pre)
        xs = (xact * sexp[:, sl]).astype(jnp.bfloat16)
        halves = []
        for k in range(2):
            h = 2 * p + k
            cumb = cumb_ref[:, pl.ds(pl.multiple_of(h * LANES, LANES), LANES)]
            cumb = jnp.concatenate([cumb] * (chunk // LANES), axis=1)
            decays = jnp.exp(cumb - cumt_ref[pl.ds(h, 1), :] + mask_ref[...])
            halves.append(dot((g_ref[...] * decays).astype(jnp.bfloat16), xs))
        inner = jnp.where(low_lane, halves[0], halves[1])
        state = sout_ref[:, sl]
        into = eexp[:, sl]
        carried = dot(cmat, state.astype(jnp.bfloat16)) * into
        fresh = dot_tn(bmat, (xact * texp[:, sl]).astype(jnp.bfloat16))
        sout_ref[:, sl] = state * into[chunk - 1 : chunk, :] + fresh
        mixbar = (inner + carried + cw[5:6, :] * xact).astype(jnp.bfloat16)
        mix_ref[:, sl] = mixbar
        gz = gate_ref[:, sl].astype(jnp.float32)
        gated = mixbar.astype(jnp.float32) * (gz * sigmoid(gz))
        gn_ref[:, sl] = (gated * cw[6:7, :]).astype(jnp.bfloat16)
        ss_ref[...] += gated * gated
        return carry

    lax.fori_loop(0, width // LANES, pair, 0)


def common_specs(chunk, width, order):
    bc_at, st_at = 2 * width // 256, (2 * width + 256) // LANES
    return [
        pl.BlockSpec((chunk, width), lambda c, perm: (perm[order(c)], 0)),
        pl.BlockSpec((chunk, width), lambda c, perm: (perm[order(c)], 1)),
        pl.BlockSpec((chunk, 256), lambda c, perm: (perm[order(c)], bc_at)),
        pl.BlockSpec((chunk, LANES), lambda c, perm: (perm[order(c)], st_at)),
    ]


def fixed(shape):
    return pl.BlockSpec(shape, lambda c, perm: (0,) * len(shape))


def last_rows(count, chunk):
    return lambda perm: (perm[count - 1] + 1) * (chunk // 16) - 1


def mixer_forward(perm, proj, before, meta, segrow, cw, cbc, hp, state, chunk=CHUNK):
    rows = proj.shape[0]
    width = cw.shape[1]
    count = rows // chunk
    same = lambda c: c
    bc_at = 2 * width // 256
    ending = last_rows(count, chunk)
    f32 = jnp.float32
    return pl.pallas_call(
        forward_kernel,
        grid_spec=pltpu.PrefetchScalarGridSpec(
        num_scalar_prefetch=1,
        grid=(count,),
        in_specs=common_specs(chunk, width, same)
        + [
            pl.BlockSpec((16, width), lambda c, perm: (ending(perm), 1)),
            pl.BlockSpec((16, 256), lambda c, perm: (ending(perm), bc_at)),
            pl.BlockSpec((chunk, 8), lambda c, perm: (c, 0)),
            pl.BlockSpec((1, 1, chunk), lambda c, perm: (c, 0, 0)),
            fixed((8, width)),
            fixed((8, 256)),
            fixed((8, LANES)),
            fixed((N, width)),
        ],
        out_specs=[
            pl.BlockSpec((chunk, width), lambda c, perm: (perm[c], 0)),
            pl.BlockSpec((chunk, width), lambda c, perm: (perm[c], 0)),
            pl.BlockSpec((chunk, LANES), lambda c, perm: (perm[c], 0)),
            pl.BlockSpec((1, N, width), lambda c, perm: (c, 0, 0)),
            fixed((N, width)),
        ],
        scratch_shapes=[
            pltpu.VMEM((chunk + 8, width), f32),
            pltpu.VMEM((chunk + 8, 256), f32),
            pltpu.VMEM((3, chunk, LANES), f32),
            pltpu.VMEM((chunk, 2 * width), f32),
            pltpu.VMEM((LANES, chunk), f32),
            pltpu.VMEM((chunk, chunk), f32),
            pltpu.VMEM((chunk, width), f32),
            pltpu.VMEM((chunk, width), f32),
            pltpu.VMEM((chunk, width), f32),
            pltpu.VMEM((LANES, width), jnp.bfloat16),
            pltpu.VMEM((LANES, 2 * width), jnp.bfloat16),
            pltpu.VMEM((chunk, chunk), f32),
        ],
        ),
        out_shape=[
            jax.ShapeDtypeStruct((rows, width), jnp.bfloat16),
            jax.ShapeDtypeStruct((rows, width), jnp.bfloat16),
            jax.ShapeDtypeStruct((rows, LANES), f32),
            jax.ShapeDtypeStruct((count, N, width), f32),
            jax.ShapeDtypeStruct((N, width), f32),
        ],
        compiler_params=pltpu.CompilerParams(
            vmem_limit_bytes=VMEM_BYTES, dimension_semantics=("arbitrary",)
        ),
        cost_estimate=pl.CostEstimate(
            flops=rows * width * 28000, bytes_accessed=rows * width * 12, transcendentals=rows * width * 6
        ),
        name="mix_fwd",
    )(perm, proj, proj, proj, proj, before, before, meta, segrow, cw, cbc, hp, state)


def conv_back(dpre, taps, masks, here, back, dpad, tail_ref, sl, chunk, acc_ref):
    acc_ref[4:5, sl] += jnp.sum(dpre, axis=0, keepdims=True)
    acc_ref[3:4, sl] += jnp.sum(dpre * here, axis=0, keepdims=True)
    grad = taps[3:4, :] * dpre
    for m in (1, 2, 3):
        acc_ref[3 - m : 4 - m, sl] += jnp.sum(dpre * back[m - 1], axis=0, keepdims=True)
        masked = dpre * masks[m - 1]
        dpad[m - 1, 0:chunk, :] = masked
        dpad[m - 1, chunk : chunk + 8, :] = tail_ref[m - 1, :, sl]
        tail_ref[m - 1, :, sl] = masked[0:8, :]
        grad = grad + taps[3 - m : 4 - m, :] * dpad[m - 1, m : m + chunk, :]
    return grad


def backward_kernel(
    perm_ref, gate_ref, x_ref, bc_ref, st_ref, px_ref, pbc_ref, hx_ref, hbc_ref, meta_ref, segrow_ref, cw_ref, cbc_ref, hp_ref,
    mix_ref, u_ref, fs_ref, states_ref, ds0_ref, tx0_ref, tbc0_ref,
    gproj_ref, acc_ref, accbc_ref, acch_ref, ds_ref, tx_ref, tbc_ref,
    xpad, bpad, masks, cumb_ref, cumt_ref, mask_ref, sexp, eexp, dexp, wide_ref, tall_ref, g_ref,
    dg_ref, db_ref, dc_ref, dcum_ref, dsx_ref, dpad, fac_ref, sb_ref,
):
    chunk, width = x_ref.shape
    step = pl.program_id(0)
    first = step == pl.num_programs(0) - 1

    @pl.when(step == 0)
    def _():
        ds_ref[...] = ds0_ref[...]
        tx_ref[...] = tx0_ref[...]
        tbc_ref[...] = tbc0_ref[...]
        acc_ref[...] = jnp.zeros_like(acc_ref)
        accbc_ref[...] = jnp.zeros_like(accbc_ref)
        acch_ref[...] = jnp.zeros_like(acch_ref)
        wide_ref[...] = spread(width, HEAD)
        tall_ref[...] = spread(width * 2, LANES)

    @pl.when(first)
    def _():
        xpad[0:8, :] = hx_ref[8:16, :].astype(jnp.float32)
        bpad[0:8, :] = hbc_ref[8:16, :].astype(jnp.float32)

    @pl.when(jnp.logical_not(first))
    def _():
        xpad[0:8, :] = px_ref[8:16, :].astype(jnp.float32)
        bpad[0:8, :] = pbc_ref[8:16, :].astype(jnp.float32)

    xpad[8 : 8 + chunk, :] = x_ref[...].astype(jnp.float32)
    bpad[8 : 8 + chunk, :] = bc_ref[...].astype(jnp.float32)
    raw, steps, cum, e, decay = chunk_setup(
        st_ref, meta_ref, segrow_ref, hp_ref, chunk, cumb_ref, cumt_ref, mask_ref, wide_ref, tall_ref
    )
    for m in range(3):
        masks[m] = jnp.broadcast_to(meta_ref[:, m : m + 1], (chunk, LANES))
    fac_ref[...] = jnp.broadcast_to(fs_ref[:, 0:1], (chunk, LANES))
    sb_ref[...] = jnp.broadcast_to(fs_ref[:, 1:2], (chunk, LANES))
    sexp[...] = dot(pack3(steps), wide_ref[...])
    eexp[...] = dot(pack3(e), wide_ref[...])
    dexp[...] = dot(pack3(decay), wide_ref[...])
    bcact, bcpre = [], []
    for half in range(2):
        sl = slice(half * LANES, (half + 1) * LANES)
        pre, back, here = conv_parts(bpad, sl, chunk, cbc_ref[:, sl], masks)
        bcact.append((pre * sigmoid(pre)).astype(jnp.bfloat16))
    bmat, cmat = bcact
    g_ref[...] = dot_nt(cmat, bmat)
    low_lane = lax.broadcasted_iota(jnp.int32, (chunk, LANES), 1) < HEAD
    last_row = lax.broadcasted_iota(jnp.int32, (chunk, LANES), 0) == chunk - 1
    dg_ref[...] = jnp.zeros_like(dg_ref)
    db_ref[...] = jnp.zeros_like(db_ref)
    dc_ref[...] = jnp.zeros_like(dc_ref)
    dcum_ref[...] = jnp.zeros_like(dcum_ref)
    dsx_ref[...] = jnp.zeros_like(dsx_ref)

    def pair(p, carry):
        start = pl.multiple_of(p * LANES, LANES)
        sl = pl.ds(start, LANES)
        cw = cw_ref[:, sl]
        gz = gate_ref[:, sl].astype(jnp.float32)
        sg = sigmoid(gz)
        active = gz * sg
        mixval = mix_ref[:, sl].astype(jnp.float32)
        gated = mixval * active
        fac = fac_ref[...]
        up = u_ref[:, sl].astype(jnp.float32) * fac
        dgated = up * cw[6:7, :] - gated * sb_ref[...]
        gm = (dgated * active).astype(jnp.bfloat16)
        gproj_ref[:, sl] = (dgated * mixval * sg * (1.0 + gz * (1.0 - sg))).astype(jnp.bfloat16)
        acc_ref[6:7, sl] += jnp.sum(gated * up, axis=0, keepdims=True)
        dy = gm.astype(jnp.float32)
        pre, back, here = conv_parts(xpad, sl, chunk, cw, masks)
        sig = sigmoid(pre)
        xact = pre * sig
        sx = sexp[:, sl]
        xs = (xact * sx).astype(jnp.bfloat16)
        xsf = xs.astype(jnp.float32)
        ys, dxs = [], []
        for k in range(2):
            h = 2 * p + k
            cumb = cumb_ref[:, pl.ds(pl.multiple_of(h * LANES, LANES), LANES)]
            cumb = jnp.concatenate([cumb] * (chunk // LANES), axis=1)
            decays = jnp.exp(cumb - cumt_ref[pl.ds(h, 1), :] + mask_ref[...])
            weights = (g_ref[...] * decays).astype(jnp.bfloat16)
            own = low_lane if k == 0 else jnp.logical_not(low_lane)
            pulls = dot_nt(jnp.where(own, dy, 0.0).astype(jnp.bfloat16), xs)
            dg_ref[...] += pulls * decays
            ys.append(dot(weights, xs))
            dxs.append(dot_tn(weights, gm))
        inner = jnp.where(low_lane, ys[0], ys[1])
        dinner = jnp.where(low_lane, dxs[0], dxs[1])
        state = states_ref[0, :, sl]
        stateb = state.astype(jnp.bfloat16)
        dstate = ds_ref[:, sl]
        dstateb = dstate.astype(jnp.bfloat16)
        into = eexp[:, sl]
        dec = dexp[:, sl]
        carried = dot(cmat, stateb) * into
        edy = (dy * into).astype(jnp.bfloat16)
        dc_ref[...] += dot_nt(edy, stateb)
        bds = dot(bmat, dstateb) * dec
        db_ref[...] += dot_nt((xsf * dec).astype(jnp.bfloat16), dstateb)
        tails = xsf * bds
        ends = jnp.sum(tails, axis=0, keepdims=True) + into[chunk - 1 : chunk, :] * jnp.sum(
            dstate * state, axis=0, keepdims=True
        )
        rowq = dy * (inner + carried) - xsf * dinner - tails + jnp.where(last_row, ends, 0.0)
        dxsum = dinner + bds
        row = lax.broadcasted_iota(jnp.int32, (LANES, LANES), 0)
        col = lax.broadcasted_iota(jnp.int32, (LANES, LANES), 1)
        gather = (col == 2 * p + row // HEAD).astype(jnp.bfloat16)
        hi, mid, lo = split3(rowq)
        dcum_ref[...] += dot(hi, gather) + dot(mid, gather) + dot(lo, gather)
        hi, mid, lo = split3(xact * dxsum)
        dsx_ref[...] += dot(hi, gather) + dot(mid, gather)
        ds_ref[:, sl] = dstate * into[chunk - 1 : chunk, :] + dot_tn(cmat, edy)
        acc_ref[5:6, sl] += jnp.sum(dy * xact, axis=0, keepdims=True)
        dact = sx * dxsum + cw[5:6, :] * dy
        dpre = dact * (sig * (1.0 + pre * (1.0 - sig)))
        grad = conv_back(dpre, cw, masks, here, back, dpad, tx_ref, sl, chunk, acc_ref)
        gproj_ref[:, pl.ds(pl.multiple_of(width + start, LANES), LANES)] = grad.astype(jnp.bfloat16)
        return carry

    lax.fori_loop(0, width // LANES, pair, 0)
    dgb = dg_ref[...].astype(jnp.bfloat16)
    grads = (db_ref[...] + dot_tn(dgb, cmat), dc_ref[...] + dot(dgb, bmat))
    for half in range(2):
        sl = slice(half * LANES, (half + 1) * LANES)
        cw = cbc_ref[:, sl]
        pre, back, here = conv_parts(bpad, sl, chunk, cw, masks)
        sig = sigmoid(pre)
        dpre = grads[half] * (sig * (1.0 + pre * (1.0 - sig)))
        grad = conv_back(dpre, cw, masks, here, back, dpad, tbc_ref, sl, chunk, accbc_ref)
        at = 2 * width + half * LANES
        gproj_ref[:, at : at + LANES] = grad.astype(jnp.bfloat16)
    row = lax.broadcasted_iota(jnp.int32, (chunk, chunk), 0)
    col = lax.broadcasted_iota(jnp.int32, (chunk, chunk), 1)
    upper = (col >= row).astype(jnp.bfloat16)
    dlogs = exact_left(upper, dcum_ref[...])
    dsteps = dsx_ref[...] + dlogs * hp_ref[1:2, :]
    draw = dsteps * sigmoid(raw)
    gproj_ref[:, 2 * width + 256 :] = draw.astype(jnp.bfloat16)
    acch_ref[0:1, :] += jnp.sum(draw, axis=0, keepdims=True)
    acch_ref[1:2, :] += jnp.sum(dlogs * steps, axis=0, keepdims=True)


def mixer_backward(perm, proj, prior, meta, segrow, cw, cbc, hp, mix, up, fs, states, dstate, tx, tbc, chunk=CHUNK):
    rows, cols = proj.shape
    width = cw.shape[1]
    count = rows // chunk
    back = lambda c: count - 1 - c
    bc_at = 2 * width // 256
    f32 = jnp.float32
    per = chunk // 16
    ending = last_rows(count, chunk)

    def before(c, perm):
        return (perm[jnp.maximum(back(c) - 1, 0)] + 1) * per - 1

    return pl.pallas_call(
        backward_kernel,
        grid_spec=pltpu.PrefetchScalarGridSpec(
        num_scalar_prefetch=1,
        grid=(count,),
        in_specs=common_specs(chunk, width, back)
        + [
            pl.BlockSpec((16, width), lambda c, perm: (before(c, perm), 1)),
            pl.BlockSpec((16, 256), lambda c, perm: (before(c, perm), bc_at)),
            pl.BlockSpec((16, width), lambda c, perm: (ending(perm), 1)),
            pl.BlockSpec((16, 256), lambda c, perm: (ending(perm), bc_at)),
            pl.BlockSpec((chunk, 8), lambda c, perm: (back(c), 0)),
            pl.BlockSpec((1, 1, chunk), lambda c, perm: (back(c), 0, 0)),
            fixed((8, width)),
            fixed((8, 256)),
            fixed((8, LANES)),
            pl.BlockSpec((chunk, width), lambda c, perm: (perm[back(c)], 0)),
            pl.BlockSpec((chunk, width), lambda c, perm: (perm[back(c)], 0)),
            pl.BlockSpec((chunk, 8), lambda c, perm: (perm[back(c)], 0)),
            pl.BlockSpec((1, N, width), lambda c, perm: (back(c), 0, 0)),
            fixed((N, width)),
            fixed((3, 8, width)),
            fixed((3, 8, 256)),
        ],
        out_specs=[
            pl.BlockSpec((chunk, cols), lambda c, perm: (perm[back(c)], 0)),
            fixed((8, width)),
            fixed((8, 256)),
            fixed((8, LANES)),
            fixed((N, width)),
            fixed((3, 8, width)),
            fixed((3, 8, 256)),
        ],
        scratch_shapes=[
            pltpu.VMEM((chunk + 8, width), f32),
            pltpu.VMEM((chunk + 8, 256), f32),
            pltpu.VMEM((3, chunk, LANES), f32),
            pltpu.VMEM((chunk, 2 * width), f32),
            pltpu.VMEM((LANES, chunk), f32),
            pltpu.VMEM((chunk, chunk), f32),
            pltpu.VMEM((chunk, width), f32),
            pltpu.VMEM((chunk, width), f32),
            pltpu.VMEM((chunk, width), f32),
            pltpu.VMEM((LANES, width), jnp.bfloat16),
            pltpu.VMEM((LANES, 2 * width), jnp.bfloat16),
            pltpu.VMEM((chunk, chunk), f32),
            pltpu.VMEM((chunk, chunk), f32),
            pltpu.VMEM((chunk, N), f32),
            pltpu.VMEM((chunk, N), f32),
            pltpu.VMEM((chunk, LANES), f32),
            pltpu.VMEM((chunk, LANES), f32),
            pltpu.VMEM((3, chunk + 8, LANES), f32),
            pltpu.VMEM((chunk, LANES), f32),
            pltpu.VMEM((chunk, LANES), f32),
        ],
        ),
        out_shape=[
            jax.ShapeDtypeStruct((rows, cols), jnp.bfloat16),
            jax.ShapeDtypeStruct((8, width), f32),
            jax.ShapeDtypeStruct((8, 256), f32),
            jax.ShapeDtypeStruct((8, LANES), f32),
            jax.ShapeDtypeStruct((N, width), f32),
            jax.ShapeDtypeStruct((3, 8, width), f32),
            jax.ShapeDtypeStruct((3, 8, 256), f32),
        ],
        compiler_params=pltpu.CompilerParams(
            vmem_limit_bytes=VMEM_BYTES, dimension_semantics=("arbitrary",)
        ),
        cost_estimate=pl.CostEstimate(
            flops=rows * width * 56000, bytes_accessed=rows * width * 24, transcendentals=rows * width * 8
        ),
        name="mix_bwd",
    )(
        perm, proj, proj, proj, proj, proj, proj, prior, prior, meta, segrow, cw, cbc, hp,
        mix, up, fs, states, dstate, tx, tbc,
    )


def token_facts(seg, chunk=CHUNK):
    total = seg.shape[0]
    place = jnp.arange(total, dtype=jnp.int32)
    cols = []
    for m in (1, 2, 3):
        before = jnp.concatenate([jnp.full((m,), -1, jnp.int32), seg[:-m]])
        cols.append(before == seg)
    ends = seg.reshape(-1, chunk)[:, -1]
    starts = jnp.concatenate([jnp.full((1,), -1, jnp.int32), ends[:-1]])
    cols.append(jnp.repeat(starts, chunk) == seg)
    cols.append(jnp.repeat(ends, chunk) == seg)
    meta = jnp.stack([c.astype(jnp.float32) for c in cols] + [seg.astype(jnp.float32)], axis=1)
    meta = jnp.pad(meta, ((0, 0), (0, 2)))
    return meta, seg.astype(jnp.float32).reshape(-1, 1, chunk)


def swap(value, axis):
    return lax.ppermute(value, axis, SWAP)


def paired():
    return lax.axis_size("x") == 2


def member_index():
    return lax.axis_index("core") * lax.axis_size("x") + lax.axis_index("x")


def slot_of(members):
    return members ^ member_index() if paired() else members


def team_gather(own, *first):
    if paired():
        came = swap(own, "x")
        row = after(jnp.concatenate([own, came]), *first)
        return jnp.concatenate([row, swap(row, "core")]), came
    row = lax.all_gather(own, "x", axis=0, tiled=True)
    other = swap(row, "core")
    first = lax.axis_index("core") == 0
    return jnp.concatenate([jnp.where(first, row, other), jnp.where(first, other, row)]), row


def team_reduce(blocks, rows, kind, first=()):
    half = lax.axis_size("x") * rows
    if paired():
        got = swap(blocks[half:], "core")
        near = blocks[rows:half].astype(jnp.float32) + got[rows:].astype(jnp.float32)
        near = after(near.astype(kind), *first)
        far = swap(near, "x")
        total = blocks[:rows].astype(jnp.float32) + got[:rows].astype(jnp.float32)
        return total + far.astype(jnp.float32), near, far
    core = lax.axis_index("core")
    halves = blocks.reshape((2, half) + blocks.shape[1:])
    got = swap(lax.dynamic_index_in_dim(halves, 1 - core, 0, False), "core")
    keep = lax.dynamic_index_in_dim(halves, core, 0, False)
    sums = (keep.astype(jnp.float32) + got.astype(jnp.float32)).astype(kind)
    total = lax.psum_scatter(sums, "x", scatter_dimension=0, tiled=True)
    return total.astype(jnp.float32), sums, total


def plane_cycle():
    across = lax.axis_size("y")
    walk = [0]
    for y in range(across):
        line = range(1, DEPTH) if y % 2 == 0 else range(DEPTH - 1, 0, -1)
        walk += [y * DEPTH + z for z in line]
    return walk + [y * DEPTH for y in range(across - 1, 0, -1)]


def plane_steps():
    walk = plane_cycle()
    count = len(walk)
    places = [walk.index(i) for i in range(count)]
    here = jnp.asarray(places, jnp.int32)[lax.axis_index("y") * DEPTH + lax.axis_index("z")]
    forwards = [(walk[i], walk[(i + 1) % count]) for i in range(count)]
    return jnp.asarray(walk, jnp.int32), here, forwards, [(b, a) for a, b in forwards]


def ring_gather(block, beside=()):
    walk, here, forwards, backwards = plane_steps()
    count = walk.shape[0]
    rows = block.shape[0]

    def put(whole, value, place):
        return lax.dynamic_update_slice_in_dim(whole, value, walk[place % count] * rows, 0)

    whole = put(jnp.zeros((count * rows, block.shape[1]), block.dtype), block, here)
    ahead = behind = block
    for step in range(1, count // 2 + 1):
        ahead = lax.ppermute(ahead, ("y", "z"), forwards)
        whole = put(whole, ahead, here + count - step)
        if step < count - count // 2:
            behind = lax.ppermute(behind, ("y", "z"), backwards)
            whole = put(whole, behind, here + step)
        if step <= len(beside):
            ahead = after(ahead, beside[step - 1])
    return whole


def deal_moves():
    moves = []
    for r in range(2):
        pairs = []
        for core in range(2):
            for z in range(DEPTH):
                pairs.append((core * DEPTH + z, (z // 2) * DEPTH + 2 * core + ((z % 2) ^ r)))
        moves.append(pairs)
    return moves


def column_blocks(across, rows):
    wide = lax.axis_size("x") * rows
    for y in range(across):
        for core in range(2):
            for z in range(DEPTH):
                yield ((y * DEPTH + z) * 2 + core) * wide, ((y * 2 + core) * DEPTH + z) * wide, wide


def to_team(rows, weight_rows):
    blocks = list(column_blocks(lax.axis_size("y"), weight_rows))
    low = lax.axis_index("z") % 2

    def body(low_ref, rows_ref, *out_refs):
        for to, at, wide in blocks:
            for r in range(2):
                out_refs[r][:, to : to + wide] = rows_ref[low_ref[0] ^ r, :, at : at + wide]

    shape = jax.ShapeDtypeStruct(rows.shape[1:], rows.dtype)
    sent = pl.pallas_call(
        body,
        grid_spec=pltpu.PrefetchScalarGridSpec(
            num_scalar_prefetch=1,
            grid=(1,),
            in_specs=[pl.BlockSpec(rows.shape, lambda c, low: (0, 0, 0))],
            out_specs=[pl.BlockSpec(rows.shape[1:], lambda c, low: (0, 0))] * 2,
        ),
        out_shape=[shape, shape],
        compiler_params=pltpu.CompilerParams(vmem_limit_bytes=VMEM_BYTES),
        name="to_plane",
    )(low.reshape(1), rows)
    return [lax.ppermute(v, ("core", "z"), pairs) for v, pairs in zip(sent, deal_moves())]


def from_team(rows):
    moves = zip(rows, deal_moves())
    return [lax.ppermute(v, ("core", "z"), [(b, a) for a, b in pairs]) for v, pairs in moves]


def dealt(got, weight_rows, kind):
    blocks = list(column_blocks(lax.axis_size("y"), weight_rows))
    low = lax.axis_index("z") % 2
    shape = got[0].shape

    def body(low_ref, first_ref, second_ref, out_ref):
        for at, to, wide in blocks:
            for r, ref in enumerate((first_ref, second_ref)):
                out_ref[low_ref[0] ^ r, :, to : to + wide] = ref[:, at : at + wide].astype(kind)

    return pl.pallas_call(
        body,
        grid_spec=pltpu.PrefetchScalarGridSpec(
            num_scalar_prefetch=1,
            grid=(1,),
            in_specs=[pl.BlockSpec(shape, lambda c, low: (0, 0))] * 2,
            out_specs=pl.BlockSpec((2,) + shape, lambda c, low: (0, 0, 0)),
        ),
        out_shape=jax.ShapeDtypeStruct((2,) + shape, kind),
        compiler_params=pltpu.CompilerParams(vmem_limit_bytes=VMEM_BYTES),
        name="to_natural",
    )(low.reshape(1), *got)


def inverse_of(perm):
    count = perm.shape[0]
    places = jnp.arange(count, dtype=jnp.int32)
    return jnp.sum(jnp.where(places[:, None] == perm[None, :], places[None, :], 0), axis=1)


def segments_of(sizes, total):
    ends = jnp.cumsum(sizes)
    places = jnp.arange(total, dtype=jnp.int32)
    return jnp.sum((places[:, None] >= ends[None, :]).astype(jnp.int32), axis=1)


def reorder(values, axis, inner, outer):
    shape = values.shape
    count = lax.axis_size("y")
    view = values.reshape(shape[:axis] + (count, inner, outer, -1) + shape[axis + 1 :])
    order = list(range(view.ndim))
    order[axis + 1], order[axis + 2] = axis + 2, axis + 1
    return view.transpose(order).reshape(shape)


def to_plane(values, axis):
    return reorder(values, axis, 2, DEPTH)


def to_members(pieces):
    sent = lax.all_to_all(pieces, ("core", "x"), split_axis=1, concat_axis=0, tiled=True)
    return sent.reshape(-1, pieces.shape[2])


def plane_gather(block):
    return lax.all_gather(block, ("y", "z"), axis=0, tiled=True)


def from_plane(summed):
    team = 2 * lax.axis_size("x")
    blocks = summed.reshape(team, -1, summed.shape[1])
    return lax.all_to_all(blocks, ("core", "x"), split_axis=0, concat_axis=0, tiled=True)


def after(value, *others):
    return lax.optimization_barrier((value,) + others)[0]


def in_kernel(layers, team, width, split_refs, weight_ref, grad_ref, norm_ref, tile_ref):
    for layer in range(layers):
        total = jnp.zeros(norm_ref.shape[1:], jnp.float32)
        pieces = []
        for q in range(team):
            pieces.append((q * width, split_refs[layer][q, :, :width].astype(jnp.float32)))
            pieces.append((DI + q * width, split_refs[layer][q, :, width : 2 * width].astype(jnp.float32)))
        states = split_refs[layer][0, :, 2 * width : 2 * width + 2 * N].astype(jnp.float32)
        for q in range(1, team):
            states = states + split_refs[layer][q, :, 2 * width : 2 * width + 2 * N].astype(jnp.float32)
        pieces.append((2 * DI, states))
        for at, value in pieces:
            count = value.shape[1]
            grad_ref[layer, :, at : at + count] = value
            product = value * weight_ref[layer, :, at : at + count].astype(jnp.float32)
            for tile in range(count // LANES):
                total = total + product[:, tile * LANES : (tile + 1) * LANES]
        tiles = split_refs[layer][:, :, 2 * width + 2 * N :].astype(jnp.float32)
        tile_ref[layer] = tiles
        count = (weight_ref.shape[2] - 2 * DI - 2 * N) // team
        steps = jnp.zeros(norm_ref.shape[1:], jnp.float32)
        lane = lax.broadcasted_iota(jnp.int32, steps.shape, 1)
        for q in range(team):
            moved = pltpu.roll(tiles[q], q * count, 1) if q else tiles[q]
            steps = jnp.where((lane >= q * count) & (lane < (q + 1) * count), moved, steps)
        grad_ref[layer, :, 2 * DI + 2 * N :] = steps[:, : team * count]
        product = steps[:, : team * count] * weight_ref[layer, :, 2 * DI + 2 * N :].astype(jnp.float32)
        norm_ref[layer] = jnp.broadcast_to(
            jnp.sum(total, axis=1, keepdims=True) + jnp.sum(product, axis=1, keepdims=True), total.shape
        )


def assemble_in(splits, in_weight):
    layers, rows, cols = in_weight.shape
    team, width = splits[0].shape[0], DI // splits[0].shape[0]

    def body(*refs):
        in_kernel(layers, team, width, refs[:layers], *refs[layers:])

    return pl.pallas_call(
        body,
        out_shape=[
            jax.ShapeDtypeStruct((layers, rows, cols), jnp.float32),
            jax.ShapeDtypeStruct((layers, rows, LANES), jnp.float32),
            jax.ShapeDtypeStruct((layers, team, rows, LANES), jnp.float32),
        ],
        compiler_params=pltpu.CompilerParams(vmem_limit_bytes=VMEM_BYTES),
        name="grad_in",
    )(*splits, in_weight)


def assemble_out(outs):
    layers = len(outs)
    team, rows, width = outs[0].shape

    def body(*refs):
        for layer in range(layers):
            for q in range(team):
                refs[layers][layer, :, q * width : (q + 1) * width] = refs[layer][q].astype(jnp.float32)

    return pl.pallas_call(
        body,
        out_shape=jax.ShapeDtypeStruct((layers, rows, DI), jnp.float32),
        compiler_params=pltpu.CompilerParams(vmem_limit_bytes=VMEM_BYTES),
        name="grad_out",
    )(*outs)


def in_columns(w_in, team, extra):
    rows = w_in.shape[0]
    bc = w_in[:, 2 * DI : 2 * DI + 2 * N]
    step = w_in[:, 2 * DI + 2 * N :].reshape(rows, team, -1)
    shared = jnp.concatenate(
        [extra, jnp.zeros((rows, LANES - step.shape[2] - extra.shape[1]), w_in.dtype)], axis=1
    )
    return jnp.concatenate(
        [
            w_in[:, :DI].reshape(rows, team, -1),
            w_in[:, DI : 2 * DI].reshape(rows, team, -1),
            jnp.broadcast_to(bc[:, None, :], (rows, team, 2 * N)),
            step,
            jnp.broadcast_to(shared[:, None, :], (rows, team, shared.shape[1])),
        ],
        axis=2,
    )


def rounded(values):
    return lax.reduce_precision(values, 8, 7)


def in_parts(values):
    hi = rounded(values)
    mid = rounded(values - hi)
    return jnp.stack([hi, mid, rounded(values - hi - mid)]).astype(jnp.bfloat16)


def as_rows(flat, rows):
    count = -(-flat.shape[-1] // rows)
    flat = jnp.pad(flat, [(0, 0)] * (flat.ndim - 1) + [(0, count * rows - flat.shape[-1])])
    return jnp.swapaxes(flat.reshape(flat.shape[:-1] + (count, rows)), -1, -2)


def row_scale(rows):
    return lax.rsqrt(jnp.mean(rows * rows, axis=1, keepdims=True) + EPS)


def per_device(
    hidden,
    lengths,
    token_order,
    norm_gain,
    in_weight,
    conv_weight,
    conv_bias,
    dt_bias,
    log_decay,
    skip_gain,
    gate_gain,
    out_weight,
    cotangent,
):
    bf16, f32 = jnp.bfloat16, jnp.float32
    layers = in_weight.shape[0]
    across = lax.axis_size("x")
    team = 2 * across
    core, z, x = (lax.axis_index(name) for name in ("core", "z", "x"))
    member = member_index()
    width = DI // team
    heads = width // HEAD
    rows_here = hidden.shape[1]
    tokens = token_order.shape[2]
    part_rows = tokens // PARTS
    own_rows = part_rows // team
    weight_rows = in_weight.shape[1]
    wide = conv_bias.shape[1]
    gate_wide = gate_gain.shape[1]
    head_wide = dt_bias.shape[1]
    bc_at = 2 * width
    step_at = bc_at + 2 * N
    extra_at = step_at + heads
    numbers = jnp.arange(tokens, dtype=jnp.int32)

    def of_pair(ints):
        return lax.dynamic_index_in_dim(
            jnp.where(z // 2 == core, ints, swap(ints, "core")), z % 2, 0, False
        )[0]

    order, sizes = of_pair(token_order), of_pair(lengths)
    inverse = inverse_of(order)
    mine = z % 2
    block, within = inverse // rows_here, inverse % rows_here
    from_z, from_x = block // across, block % across
    place = (slot_of(from_z // 2 * across + from_x) * 2 + (from_z % 2 ^ mine)) * rows_here + within
    if paired():
        view = place.reshape(PARTS, 2, 2, own_rows)
        view = jnp.where(core == 1, view[:, ::-1], view)
        place = jnp.where(x == 1, view[:, :, ::-1], view).reshape(-1)
    target = jnp.concatenate(
        [
            lax.dynamic_slice_in_dim(order, ((2 * core + (r ^ mine)) * across + x) * rows_here, rows_here)
            for r in range(2)
        ]
    )
    inside = target % part_rows
    own_place = (
        target // part_rows * part_rows + slot_of(inside // own_rows) * own_rows + inside % own_rows
    )
    meta, segrow = token_facts(segments_of(sizes, tokens))
    chunks = numbers[: part_rows // CHUNK]
    if paired():
        per = own_rows // CHUNK
        perm = slot_of(chunks // per) * per + chunks % per
    else:
        perm = chunks

    small = []
    for layer in range(layers):
        per_head = jnp.stack([dt_bias[layer], log_decay[layer], skip_gain[layer]])
        flat = [conv_weight[layer], conv_bias[layer], gate_gain[layer], in_parts(per_head)]
        flat = as_rows(jnp.concatenate([v.reshape(-1) for v in flat]), weight_rows)
        small.append(jnp.concatenate([norm_gain[layer][:, None], flat], axis=1))
    extras = small[0].shape[1]
    def part(values, i):
        return values[i * part_rows : (i + 1) * part_rows]

    places = [part(place, i) for i in range(PARTS)]
    arrived = to_team(hidden, weight_rows)
    sent_in = to_members(in_columns(in_weight[0], team, small[0]))
    pieces = [out_weight[layer].T.reshape(-1, team, width) for layer in range(layers)]
    pieces += [in_columns(in_weight[layer], team, small[layer]) for layer in range(1, layers)]
    blocks = to_members(after(jnp.concatenate(pieces, axis=2), sent_in))
    gathered, came = team_gather(jnp.concatenate(arrived))
    w_cols = [ring_gather(sent_in, (blocks, came, gathered))]
    everything = [gathered[at] for at in places]
    w_out = [plane_gather(blocks[:, :width])]
    arrived_out = to_team(after(cotangent, everything[0]), weight_rows)
    gout_gathered, came_out = team_gather(jnp.concatenate(arrived_out))
    cols = sent_in.shape[1]
    for layer in range(1, layers):
        start = layers * width + (layer - 1) * cols
        w_cols.append(plane_gather(after(blocks[:, start : start + cols], gathered)))
        block = blocks[:, layer * width : (layer + 1) * width]
        w_out.append(plane_gather(after(block, everything[0])))

    def own_columns(values):
        return lax.dynamic_slice_in_dim(values, member * width, width, values.ndim - 1)

    def tables_of(tile):
        spare = tile.astype(f32).T[heads : heads + extras]
        gain = spare[0]
        flat = spare[1:].reshape(extras - 1, -1, weight_rows).transpose(1, 0, 2)
        flat = flat.reshape(-1, DEPTH, 2, across, weight_rows * (extras - 1))
        heads_flat = flat[0, :, 0, :, (CONV + 1) * wide + gate_wide :][:, :, : 9 * head_wide]
        per_head = jnp.sum(heads_flat.astype(f32).reshape(-1, 3, 3, head_wide), axis=1)
        per_head = per_head.transpose(1, 0, 2).reshape(3, -1)
        own_heads = lax.dynamic_slice_in_dim(per_head, member * heads, heads, 1)
        flat = flat.transpose(0, 2, 1, 3, 4).reshape(-1, weight_rows * (extras - 1)).astype(f32)
        taps = flat[:, : CONV * wide].reshape(-1, CONV, wide).transpose(1, 0, 2).reshape(CONV, -1)
        shift = flat[:, CONV * wide : (CONV + 1) * wide].reshape(1, -1)
        ggain = flat[:, (CONV + 1) * wide : (CONV + 1) * wide + gate_wide].reshape(1, -1)
        cw = jnp.concatenate(
            [
                own_columns(taps[:, :DI]),
                own_columns(shift[:, :DI]),
                jnp.repeat(own_heads[2], HEAD)[None],
                own_columns(ggain),
                jnp.zeros((1, width), f32),
            ]
        )
        cbc = jnp.concatenate([taps[:, DI:], shift[:, DI:], jnp.zeros((3, 2 * N), f32)])
        hp = jnp.stack([own_heads[0], -jnp.exp(own_heads[1])])
        return gain, (cw, cbc, jnp.pad(hp, ((0, 6), (0, LANES - heads))))

    def facts(i):
        count = part_rows // CHUNK
        return part(meta, i), segrow[i * count : (i + 1) * count]

    def own_first(values):
        start = 0 if paired() else member * own_rows
        return lax.dynamic_slice_in_dim(values, start, own_rows, 0)

    states = [own_first(everything[i]).astype(f32) for i in range(PARTS)]
    record = []
    last = []

    def turn(value, *needed):
        return after(value, *last, *needed)

    def done(value):
        last[:] = [value]
        return value

    ready, needed = tuple(arrived_out), ()
    tables, gains, own_normed, gathered_rows = [], [], [None] * PARTS, [None] * PARTS

    def normed_rows(rows, gain, *before):
        rows = after(rows, *before)
        return (rows * row_scale(rows) * gain).astype(bf16)

    for layer in range(layers):
        gain, table = tables_of(turn(w_cols[layer][:, step_at:]))
        gains.append(gain)
        tables.append(table)
        kept = []
        state = jnp.zeros((N, width), f32)
        before = None
        for i in range(PARTS):
            rows = states[i]
            if layer == 0:
                normed = normed_rows(everything[i].astype(f32), gain)
            else:
                normed = gathered_rows[i]
            proj = jnp.dot(turn(normed), w_cols[layer], preferred_element_type=f32).astype(bf16)
            done(proj)
            before = proj if before is None else before
            mix, gated, squares, starts, state = mixer_forward(
                perm, turn(proj, *ready), before, *facts(i), *table, state
            )
            done(gated)
            partial = done(dot_nt(turn(gated, *needed), w_out[layer]).astype(bf16))
            total, sent_total, far_total = team_reduce(jnp.sum(squares, axis=1), own_rows, f32)
            branch, sent, far = team_reduce(partial, own_rows, bf16, (far_total,))
            factor = lax.rsqrt(total / DI + EPS)
            states[i] = rows + branch * factor[:, None]
            ready, needed = (sent,), (far,)
            if layer + 1 < layers:
                later = tables_of(w_cols[layer + 1][:, step_at:])[0]
                own_normed[i] = normed_rows(states[i], later, *own_normed[:i])
                gathered_rows[i], _ = team_gather(own_normed[i])
                needed = (own_normed[i],)
            if layer == 0 and i == 0:
                ready += (came_out,)
            if layer == 0 and i == PARTS - 1:
                rows_at = turn(gout_gathered)
                gout_parts = [rows_at[at] for at in places]
                ready += tuple(gout_parts)
            kept.append((rows, normed, proj, before, mix, starts, branch.astype(bf16), factor, gated))
            before = proj
        record.append(kept)

    def with_small(sum_in, sums, layer):
        acc, acc_bc, acc_h = sums
        taps_full = jnp.zeros((CONV + 1, DI + 2 * N), f32)
        taps_full = lax.dynamic_update_slice(taps_full, acc[: CONV + 1], (0, member * width))
        taps_full = lax.dynamic_update_slice(taps_full, acc_bc[: CONV + 1], (0, DI))
        gate_full = lax.dynamic_update_slice(jnp.zeros((DI,), f32), acc[6], (member * width,))
        head_sums = jnp.stack(
            [
                acc_h[0, :heads],
                acc_h[1, :heads] * tables[layer][2][1, :heads],
                jnp.sum(acc[5].reshape(heads, HEAD), axis=1),
            ]
        )
        head_full = lax.dynamic_update_slice(
            jnp.zeros((3, team * heads), f32), head_sums, (0, member * heads)
        )
        head_full = head_full.reshape(3, -1, head_wide).transpose(1, 0, 2).reshape(-1, 3 * head_wide)
        owners = 2 * lax.axis_size("y")
        flat = jnp.concatenate(
            [
                taps_full.reshape(CONV + 1, -1, wide).transpose(1, 0, 2).reshape(-1, (CONV + 1) * wide),
                gate_full.reshape(-1, gate_wide),
                jnp.tile(head_full, (owners, 1)),
            ],
            axis=1,
        )
        flat = as_rows(to_plane(flat, 0), weight_rows)
        spare = flat.shape[-1]
        flat = flat.reshape(-1, spare).astype(bf16)
        tile = jnp.concatenate(
            [
                sum_in[:, step_at:extra_at],
                flat,
                jnp.zeros((flat.shape[0], LANES - heads - spare), bf16),
            ],
            axis=1,
        )
        return lax.dynamic_update_slice(sum_in, tile, (0, step_at))

    def picked(parts):
        return jnp.concatenate(parts)[own_place].reshape(2, rows_here, -1)

    grads_rows = [own_first(gout_parts[i]).astype(f32) for i in range(PARTS)]

    def gather_rows(values):
        return team_gather(values[None])[0].reshape(part_rows)

    factors = [[gather_rows(record[layer][i][7]) for i in range(PARTS)] for layer in range(layers)]

    def scales_of(layer, i):
        branch, factor = record[layer][i][6:8]
        inner = jnp.sum(grads_rows[i].astype(bf16).astype(f32) * branch.astype(f32), axis=1)
        pulls = gather_rows(factor * factor * factor * inner / DI)
        return jnp.pad(jnp.stack([factors[layer][i], pulls], axis=1), ((0, 0), (0, 6)))

    def pull_in(layer, i, gout, scales, *needed):
        up = done(jnp.dot(turn(gout), w_out[layer], preferred_element_type=f32).astype(bf16))
        rows, normed, proj, before, mix, starts = record[layer][i][:6]
        found = mixer_backward(
            perm, proj, before, *facts(i), *tables[layer], mix, turn(up, *needed), scales, starts, *carry[0]
        )
        done(found[0])
        carry[0] = found[4:]
        carry[1] = found[1:4] if carry[1] is None else tuple(a + b for a, b in zip(carry[1], found[1:4]))
        return found[0]

    def send_back(layer, gproj, *needed):
        partial = done(dot_nt(turn(gproj, *needed), w_cols[layer]).astype(bf16))
        return team_reduce(partial, own_rows, bf16)

    def add_in(layer, i, gproj, total, *needed):
        term = dot_tn(record[layer][i][1], turn(gproj, *needed))
        return done((term if total is None else term + total.astype(f32)).astype(bf16))

    def add_out(layer, i, gout, total, *needed):
        scaled = record[layer][i][8].astype(f32) * factors[layer][i][:, None]
        term = dot_tn(turn(gout, *needed), scaled.astype(bf16))
        return done((term if total is None else term + total.astype(f32)).astype(bf16))

    def step_back(layer, i, gnormed):
        rows = record[layer][i][0]
        scale = row_scale(rows)
        pulled = gnormed * gains[layer]
        back = jnp.mean(pulled * rows, axis=1, keepdims=True)
        return grads_rows[i] + scale * pulled - rows * (scale * scale * scale * back)

    def plane_sum(values):
        return lax.psum_scatter(values, ("y", "z"), scatter_dimension=0, tiled=True)

    carry = [None, None]
    splits, outs = [None] * layers, [None] * layers
    gouts = list(gout_parts)
    top = layers - 1
    sum_out = None
    for i in reversed(range(PARTS)):
        sum_out = add_out(top, i, gouts[i], sum_out)
    sum_out_done = plane_sum(sum_out)
    outs[top] = from_plane(sum_out_done)
    scales = [scales_of(top, i) for i in range(PARTS)]
    sent, pending = (), None
    out_parts = [None] * PARTS

    def catch_up(pending, *started):
        layer, i, gnormed = pending
        grads_rows[i] = step_back(layer, i, after(gnormed, *started))
        own = grads_rows[i].astype(bf16)
        if layer > 0:
            next_gouts[i] = team_gather(own)
            next_scales[i] = scales_of(layer - 1, i)
        else:
            last_rows_of[i] = team_gather(own)
        return (own,)

    last_rows_of = [None] * PARTS
    next_gouts, next_scales = gouts, scales
    for layer in reversed(range(layers)):
        carry[:] = [
            (jnp.zeros((N, width), f32), jnp.zeros((3, 8, width), f32), jnp.zeros((3, 8, 2 * N), f32)),
            None,
        ]
        sum_in, sum_out, kept = None, None, [None] * PARTS
        if layer == top:
            next_gouts, next_scales = [None] * PARTS, [None] * PARTS
        for i in reversed(range(PARTS)):
            if layer < top:
                gouts[i], scales[i] = next_gouts[i][0], next_scales[i]
            gproj = pull_in(layer, i, gouts[i], scales[i], *sent)
            kept[i] = gproj
            needed = catch_up(pending, gproj) if pending is not None else ()
            if layer == top:
                out_parts[i], came = team_gather(after(states[i].astype(bf16), gproj))
                if i + 1 < PARTS:
                    needed += (out_parts[i + 1],)
            if layer == 0 and i == 0:
                sum_in = add_in(layer, i, gproj, sum_in, *needed, *splits[1:], *outs[1:])
                sum_in = done(with_small(sum_in, carry[1], layer))
                splits[layer] = plane_sum(sum_in)
            gnormed, near, far = send_back(layer, gproj, *needed)
            sent, pending = (near,), (layer, i, gnormed)
            if layer == 0 and i > 0:
                sum_out = add_out(layer, i, gouts[i], sum_out)
                sum_in = add_in(layer, i, gproj, sum_in, next_gouts[i - 1][1])
                sum_out = add_out(layer, i - 1, next_gouts[i - 1][0], sum_out)
                summed_out = plane_sum(sum_out)
        if layer > 0:
            for i in reversed(range(PARTS)):
                wait = (next_gouts[i + 1][1], sum_out_done) if i + 1 < PARTS else ()
                sum_in = add_in(layer, i, kept[i], sum_in, *wait)
            sum_in = done(with_small(sum_in, carry[1], layer))
            splits[layer] = from_plane(plane_sum(sum_in))
        else:
            outs[layer] = from_plane(summed_out)
    block_out = from_team(picked([after(p, *last) for p in out_parts]))
    catch_up(pending)
    rows = picked([p[0] for p in last_rows_of])
    block_out = dealt(block_out, weight_rows, bf16)
    grad_hidden = dealt(from_team(rows), weight_rows, f32)
    splits[0] = from_plane(after(splits[0], block_out, grad_hidden))
    grad_out = assemble_out(outs).transpose(0, 2, 1)
    grad_in, products, tiles = assemble_in(splits, in_weight)
    spare = extras - 1
    sums = jnp.sum(tiles, axis=1).transpose(0, 2, 1)[:, heads : heads + spare].reshape(layers, -1)
    shift_at, gate_at, head_at = CONV * wide, (CONV + 1) * wide, (CONV + 1) * wide + gate_wide
    grad_heads = sums[:, head_at : head_at + 3 * head_wide].reshape(layers, 3, head_wide)
    return (
        block_out,
        grad_hidden,
        products[:, :, 0] / norm_gain.astype(f32),
        grad_in,
        sums[:, :shift_at].reshape(layers, CONV, wide),
        sums[:, shift_at:gate_at],
        grad_heads[:, 0],
        grad_heads[:, 1],
        grad_heads[:, 2],
        sums[:, gate_at:head_at],
        grad_out,
    )


def solution(mesh):
    grid = mesh.devices.reshape(mesh.shape["dp"] // 2, 2, DEPTH, mesh.shape["seq"] // DEPTH)
    fine = Mesh(grid, ("y", "core", "z", "x"))
    dp, seq = ("y", "core"), ("z", "x")
    both = dp + seq
    return jax.shard_map(
        per_device,
        mesh=fine,
        in_specs=(
            P(None, both, None),
            P(None, dp, None),
            P(None, dp, None),
            P(None, both),
            P(None, both, None),
            P(None, None, both),
            P(None, both),
            P(None, seq),
            P(None, seq),
            P(None, seq),
            P(None, both),
            P(None, None, both),
            P(None, both, None),
        ),
        out_specs=(
            P(None, both, None),
            P(None, both, None),
            P(None, both),
            P(None, both, None),
            P(None, None, both),
            P(None, both),
            P(None, seq),
            P(None, seq),
            P(None, seq),
            P(None, both),
            P(None, None, both),
        ),
        check_vma=False,
    )
```

```python
import jax
import jax.numpy as jnp
from jax import lax
from jax.experimental import pallas as pl
from jax.experimental.pallas import tpu as pltpu
from jax.sharding import Mesh
from jax.sharding import PartitionSpec as P

DI = 4096
N = 128
CONV = 4
EPS = 1e-05
PARTS = 2
DEPTH = 4
SWAP = ((0, 1), (1, 0))
CHUNK = 256
LANES = 128
HEAD = 64
FAR = -1e30
VMEM_BYTES = 52 * 1024 * 1024


def sigmoid(v):
    return 0.5 * jnp.tanh(0.5 * v) + 0.5


def dot(a, b):
    return jnp.dot(a, b, preferred_element_type=jnp.float32)


def dot_nt(a, b):
    return lax.dot_general(a, b, (((1,), (1,)), ((), ())), preferred_element_type=jnp.float32)


def dot_tn(a, b):
    return lax.dot_general(a, b, (((0,), (0,)), ((), ())), preferred_element_type=jnp.float32)


def split3(v):
    hi = v.astype(jnp.bfloat16)
    rest = v - hi.astype(jnp.float32)
    mid = rest.astype(jnp.bfloat16)
    lo = (rest - mid.astype(jnp.float32)).astype(jnp.bfloat16)
    return hi, mid, lo


def pack3(v):
    hi, mid, lo = split3(v)
    lane = lax.broadcasted_iota(jnp.int32, v.shape, 1)
    mid = pltpu.roll(mid.astype(jnp.float32), 32, 1)
    lo = pltpu.roll(lo.astype(jnp.float32), 64, 1)
    joined = jnp.where(
        lane < 32, hi.astype(jnp.float32), jnp.where(lane < 64, mid, jnp.where(lane < 96, lo, 0.0))
    )
    return joined.astype(jnp.bfloat16)


def spread(rows_width, per):
    row = lax.broadcasted_iota(jnp.int32, (LANES, rows_width), 0)
    col = lax.broadcasted_iota(jnp.int32, (LANES, rows_width), 1)
    return ((row < 96) & (row % 32 == col // per)).astype(jnp.bfloat16)


def exact_left(matrix, v):
    hi, mid, lo = split3(v)
    return dot(matrix, hi) + dot(matrix, mid) + dot(matrix, lo)


def chunk_setup(st_ref, meta_ref, segrow_ref, hp_ref, chunk, cumb_ref, cumt_ref, mask_ref, wide_ref, tall_ref):
    raw = st_ref[...].astype(jnp.float32) + hp_ref[0:1, :]
    steps = jnp.maximum(raw, 0.0) + jnp.log1p(jnp.exp(-jnp.abs(raw)))
    row = lax.broadcasted_iota(jnp.int32, (chunk, chunk), 0)
    col = lax.broadcasted_iota(jnp.int32, (chunk, chunk), 1)
    lower = (row >= col).astype(jnp.bfloat16)
    cum = exact_left(lower, steps * hp_ref[1:2, :])
    cumb_ref[...] = dot(pack3(cum), tall_ref[...])
    cumt_ref[...] = cum.T
    seg = meta_ref[:, 5:6]
    same = jnp.broadcast_to(seg, (chunk, chunk)) == segrow_ref[0]
    mask_ref[...] = jnp.where(same & (row >= col), 0.0, FAR)
    e = jnp.exp(cum) * meta_ref[:, 3:4]
    decay = jnp.exp(cum[chunk - 1 : chunk, :] - cum) * meta_ref[:, 4:5]
    return raw, steps, cum, e, decay


def row_blocks(chunk):
    return [(at, at + LANES) for at in range(0, chunk, LANES)]


def block_decays(cumb, cumt, mask_ref, top, end):
    rows = jnp.concatenate([cumb[top:end]] * (end // LANES), axis=1)
    return jnp.exp(rows - cumt[:, :end] + mask_ref[top:end, :end])


def conv_parts(pad_ref, sl, chunk, cw, masks):
    here = pad_ref[8 : 8 + chunk, sl]
    back = [pad_ref[8 - m : 8 - m + chunk, sl] * masks[m - 1] for m in (1, 2, 3)]
    pre = cw[4:5, :] + cw[3:4, :] * here
    for m in (1, 2, 3):
        pre = pre + cw[3 - m : 4 - m, :] * back[m - 1]
    return pre, back, here


def forward_kernel(
    perm_ref, gate_ref, x_ref, bc_ref, st_ref, hx_ref, hbc_ref, meta_ref, segrow_ref, cw_ref, cbc_ref, hp_ref, s0_ref,
    mix_ref, gn_ref, ss_ref, states_ref, sout_ref,
    xpad, bpad, masks, cumb_ref, cumt_ref, mask_ref, sexp, eexp, texp, wide_ref, tall_ref, g_ref,
):
    chunk, width = x_ref.shape
    step = pl.program_id(0)

    @pl.when(step == 0)
    def _():
        sout_ref[...] = s0_ref[...]
        xpad[0:8, :] = hx_ref[8:16, :].astype(jnp.float32)
        bpad[0:8, :] = hbc_ref[8:16, :].astype(jnp.float32)
        wide_ref[...] = spread(width, HEAD)
        tall_ref[...] = spread(width * 2, LANES)

    @pl.when(step > 0)
    def _():
        xpad[0:8, :] = xpad[chunk : chunk + 8, :]
        bpad[0:8, :] = bpad[chunk : chunk + 8, :]

    xpad[8 : 8 + chunk, :] = x_ref[...].astype(jnp.float32)
    bpad[8 : 8 + chunk, :] = bc_ref[...].astype(jnp.float32)
    states_ref[0] = sout_ref[...]
    raw, steps, cum, e, decay = chunk_setup(
        st_ref, meta_ref, segrow_ref, hp_ref, chunk, cumb_ref, cumt_ref, mask_ref, wide_ref, tall_ref
    )
    for m in range(3):
        masks[m] = jnp.broadcast_to(meta_ref[:, m : m + 1], (chunk, LANES))
    sexp[...] = dot(pack3(steps), wide_ref[...])
    eexp[...] = dot(pack3(e), wide_ref[...])
    texp[...] = dot(pack3(decay * steps), wide_ref[...])
    bcact = []
    for half in range(2):
        sl = slice(half * LANES, (half + 1) * LANES)
        pre, _, _ = conv_parts(bpad, sl, chunk, cbc_ref[:, sl], masks)
        bcact.append((pre * sigmoid(pre)).astype(jnp.bfloat16))
    bmat, cmat = bcact
    g_ref[...] = dot_nt(cmat, bmat)
    low_lane = lax.broadcasted_iota(jnp.int32, (chunk, LANES), 1) < HEAD
    ss_ref[...] = jnp.zeros_like(ss_ref)

    def pair(p, carry):
        start = pl.multiple_of(p * LANES, LANES)
        sl = pl.ds(start, LANES)
        cw = cw_ref[:, sl]
        pre, _, _ = conv_parts(xpad, sl, chunk, cw, masks)
        xact = pre * sigmoid(pre)
        xs = (xact * sexp[:, sl]).astype(jnp.bfloat16)
        halves = []
        for k in range(2):
            h = 2 * p + k
            cumb = cumb_ref[:, pl.ds(pl.multiple_of(h * LANES, LANES), LANES)]
            cumt = cumt_ref[pl.ds(h, 1), :]
            parts = []
            for top, end in row_blocks(chunk):
                decays = block_decays(cumb, cumt, mask_ref, top, end)
                weights = (g_ref[top:end, :end] * decays).astype(jnp.bfloat16)
                parts.append(dot(weights, xs[:end]))
            halves.append(jnp.concatenate(parts))
        inner = jnp.where(low_lane, halves[0], halves[1])
        state = sout_ref[:, sl]
        into = eexp[:, sl]
        carried = dot(cmat, state.astype(jnp.bfloat16)) * into
        fresh = dot_tn(bmat, (xact * texp[:, sl]).astype(jnp.bfloat16))
        sout_ref[:, sl] = state * into[chunk - 1 : chunk, :] + fresh
        mixbar = (inner + carried + cw[5:6, :] * xact).astype(jnp.bfloat16)
        mix_ref[:, sl] = mixbar
        gz = gate_ref[:, sl].astype(jnp.float32)
        gated = mixbar.astype(jnp.float32) * (gz * sigmoid(gz))
        gn_ref[:, sl] = (gated * cw[6:7, :]).astype(jnp.bfloat16)
        ss_ref[...] += gated * gated
        return carry

    lax.fori_loop(0, width // LANES, pair, 0, unroll=4)


def common_specs(chunk, width, order):
    bc_at, st_at = 2 * width // 256, (2 * width + 256) // LANES
    return [
        pl.BlockSpec((chunk, width), lambda c, perm: (perm[order(c)], 0)),
        pl.BlockSpec((chunk, width), lambda c, perm: (perm[order(c)], 1)),
        pl.BlockSpec((chunk, 256), lambda c, perm: (perm[order(c)], bc_at)),
        pl.BlockSpec((chunk, LANES), lambda c, perm: (perm[order(c)], st_at)),
    ]


def fixed(shape):
    return pl.BlockSpec(shape, lambda c, perm: (0,) * len(shape))


def last_rows(count, chunk):
    return lambda perm: (perm[count - 1] + 1) * (chunk // 16) - 1


def mixer_forward(perm, proj, before, meta, segrow, cw, cbc, hp, state, chunk=CHUNK):
    rows = proj.shape[0]
    width = cw.shape[1]
    count = rows // chunk
    same = lambda c: c
    bc_at = 2 * width // 256
    ending = last_rows(count, chunk)
    f32 = jnp.float32
    return pl.pallas_call(
        forward_kernel,
        grid_spec=pltpu.PrefetchScalarGridSpec(
        num_scalar_prefetch=1,
        grid=(count,),
        in_specs=common_specs(chunk, width, same)
        + [
            pl.BlockSpec((16, width), lambda c, perm: (ending(perm), 1)),
            pl.BlockSpec((16, 256), lambda c, perm: (ending(perm), bc_at)),
            pl.BlockSpec((chunk, 8), lambda c, perm: (c, 0)),
            pl.BlockSpec((1, 1, chunk), lambda c, perm: (c, 0, 0)),
            fixed((8, width)),
            fixed((8, 256)),
            fixed((8, LANES)),
            fixed((N, width)),
        ],
        out_specs=[
            pl.BlockSpec((chunk, width), lambda c, perm: (perm[c], 0)),
            pl.BlockSpec((chunk, width), lambda c, perm: (perm[c], 0)),
            pl.BlockSpec((chunk, LANES), lambda c, perm: (perm[c], 0)),
            pl.BlockSpec((1, N, width), lambda c, perm: (c, 0, 0)),
            fixed((N, width)),
        ],
        scratch_shapes=[
            pltpu.VMEM((chunk + 8, width), f32),
            pltpu.VMEM((chunk + 8, 256), f32),
            pltpu.VMEM((3, chunk, LANES), f32),
            pltpu.VMEM((chunk, 2 * width), f32),
            pltpu.VMEM((LANES, chunk), f32),
            pltpu.VMEM((chunk, chunk), f32),
            pltpu.VMEM((chunk, width), f32),
            pltpu.VMEM((chunk, width), f32),
            pltpu.VMEM((chunk, width), f32),
            pltpu.VMEM((LANES, width), jnp.bfloat16),
            pltpu.VMEM((LANES, 2 * width), jnp.bfloat16),
            pltpu.VMEM((chunk, chunk), f32),
        ],
        ),
        out_shape=[
            jax.ShapeDtypeStruct((rows, width), jnp.bfloat16),
            jax.ShapeDtypeStruct((rows, width), jnp.bfloat16),
            jax.ShapeDtypeStruct((rows, LANES), f32),
            jax.ShapeDtypeStruct((count, N, width), f32),
            jax.ShapeDtypeStruct((N, width), f32),
        ],
        compiler_params=pltpu.CompilerParams(
            vmem_limit_bytes=VMEM_BYTES, dimension_semantics=("arbitrary",)
        ),
        cost_estimate=pl.CostEstimate(
            flops=rows * width * 28000, bytes_accessed=rows * width * 12, transcendentals=rows * width * 6
        ),
        name="mix_fwd",
    )(perm, proj, proj, proj, proj, before, before, meta, segrow, cw, cbc, hp, state)


def conv_back(dpre, taps, masks, here, back, dpad, tail_ref, sl, chunk, acc_ref):
    acc_ref[4:5, sl] += jnp.sum(dpre, axis=0, keepdims=True)
    acc_ref[3:4, sl] += jnp.sum(dpre * here, axis=0, keepdims=True)
    grad = taps[3:4, :] * dpre
    for m in (1, 2, 3):
        acc_ref[3 - m : 4 - m, sl] += jnp.sum(dpre * back[m - 1], axis=0, keepdims=True)
        masked = dpre * masks[m - 1]
        dpad[m - 1, 0:chunk, :] = masked
        dpad[m - 1, chunk : chunk + 8, :] = tail_ref[m - 1, :, sl]
        tail_ref[m - 1, :, sl] = masked[0:8, :]
        grad = grad + taps[3 - m : 4 - m, :] * dpad[m - 1, m : m + chunk, :]
    return grad


def backward_kernel(
    perm_ref, gate_ref, x_ref, bc_ref, st_ref, px_ref, pbc_ref, hx_ref, hbc_ref, meta_ref, segrow_ref, cw_ref, cbc_ref, hp_ref,
    mix_ref, u_ref, fs_ref, states_ref, ds0_ref, tx0_ref, tbc0_ref,
    gproj_ref, acc_ref, accbc_ref, acch_ref, ds_ref, tx_ref, tbc_ref,
    xpad, bpad, masks, cumb_ref, cumt_ref, mask_ref, sexp, eexp, dexp, wide_ref, tall_ref, g_ref,
    dg_ref, dcb_ref, dcum_ref, dpad, fac_ref, sb_ref,
):
    chunk, width = x_ref.shape
    step = pl.program_id(0)
    first = step == pl.num_programs(0) - 1

    @pl.when(step == 0)
    def _():
        ds_ref[...] = ds0_ref[...]
        tx_ref[...] = tx0_ref[...]
        tbc_ref[...] = tbc0_ref[...]
        acc_ref[...] = jnp.zeros_like(acc_ref)
        accbc_ref[...] = jnp.zeros_like(accbc_ref)
        acch_ref[...] = jnp.zeros_like(acch_ref)
        wide_ref[...] = spread(width, HEAD)
        tall_ref[...] = spread(width * 2, LANES)

    @pl.when(first)
    def _():
        xpad[0:8, :] = hx_ref[8:16, :].astype(jnp.float32)
        bpad[0:8, :] = hbc_ref[8:16, :].astype(jnp.float32)

    @pl.when(jnp.logical_not(first))
    def _():
        xpad[0:8, :] = px_ref[8:16, :].astype(jnp.float32)
        bpad[0:8, :] = pbc_ref[8:16, :].astype(jnp.float32)

    xpad[8 : 8 + chunk, :] = x_ref[...].astype(jnp.float32)
    bpad[8 : 8 + chunk, :] = bc_ref[...].astype(jnp.float32)
    raw, steps, cum, e, decay = chunk_setup(
        st_ref, meta_ref, segrow_ref, hp_ref, chunk, cumb_ref, cumt_ref, mask_ref, wide_ref, tall_ref
    )
    for m in range(3):
        masks[m] = jnp.broadcast_to(meta_ref[:, m : m + 1], (chunk, LANES))
    fac_ref[...] = jnp.broadcast_to(fs_ref[:, 0:1], (chunk, LANES))
    sb_ref[...] = jnp.broadcast_to(fs_ref[:, 1:2], (chunk, LANES))
    sexp[...] = dot(pack3(steps), wide_ref[...])
    eexp[...] = dot(pack3(e), wide_ref[...])
    dexp[...] = dot(pack3(decay), wide_ref[...])
    bcact, bcpre = [], []
    for half in range(2):
        sl = slice(half * LANES, (half + 1) * LANES)
        pre, back, here = conv_parts(bpad, sl, chunk, cbc_ref[:, sl], masks)
        bcact.append((pre * sigmoid(pre)).astype(jnp.bfloat16))
    bmat, cmat = bcact
    g_ref[...] = dot_nt(cmat, bmat)
    low_lane = lax.broadcasted_iota(jnp.int32, (chunk, LANES), 1) < HEAD
    last_row = lax.broadcasted_iota(jnp.int32, (chunk, LANES), 0) == chunk - 1
    dg_ref[...] = jnp.zeros_like(dg_ref)
    dcb_ref[...] = jnp.zeros_like(dcb_ref)
    dcum_ref[...] = jnp.zeros_like(dcum_ref)
    cbmat = jnp.concatenate([cmat, bmat], axis=1)

    def pair(p, carry):
        start = pl.multiple_of(p * LANES, LANES)
        sl = pl.ds(start, LANES)
        cw = cw_ref[:, sl]
        gz = gate_ref[:, sl].astype(jnp.float32)
        sg = sigmoid(gz)
        active = gz * sg
        mixval = mix_ref[:, sl].astype(jnp.float32)
        gated = mixval * active
        fac = fac_ref[...]
        up = u_ref[:, sl].astype(jnp.float32) * fac
        dgated = up * cw[6:7, :] - gated * sb_ref[...]
        gm = (dgated * active).astype(jnp.bfloat16)
        gproj_ref[:, sl] = (dgated * mixval * sg * (1.0 + gz * (1.0 - sg))).astype(jnp.bfloat16)
        acc_ref[6:7, sl] += jnp.sum(gated * up, axis=0, keepdims=True)
        dy = gm.astype(jnp.float32)
        pre, back, here = conv_parts(xpad, sl, chunk, cw, masks)
        sig = sigmoid(pre)
        xact = pre * sig
        sx = sexp[:, sl]
        xs = (xact * sx).astype(jnp.bfloat16)
        xsf = xs.astype(jnp.float32)
        ys, dxs = [], []
        for k in range(2):
            h = 2 * p + k
            cumb = cumb_ref[:, pl.ds(pl.multiple_of(h * LANES, LANES), LANES)]
            cumt = cumt_ref[pl.ds(h, 1), :]
            own = low_lane if k == 0 else jnp.logical_not(low_lane)
            dyown = jnp.where(own, dy, 0.0).astype(jnp.bfloat16)
            parts, total = [], None
            for top, end in reversed(row_blocks(chunk)):
                decays = block_decays(cumb, cumt, mask_ref, top, end)
                weights = (g_ref[top:end, :end] * decays).astype(jnp.bfloat16)
                dg_ref[top:end, :end] += dot_nt(dyown[top:end], xs[:end]) * decays
                parts.insert(0, dot(weights, xs[:end]))
                found = dot_tn(weights, gm[top:end])
                if total is None:
                    total = found
                else:
                    total = jnp.concatenate([total[:end] + found, total[end:]])
            ys.append(jnp.concatenate(parts))
            dxs.append(total)
        inner = jnp.where(low_lane, ys[0], ys[1])
        dinner = jnp.where(low_lane, dxs[0], dxs[1])
        state = states_ref[0, :, sl]
        stateb = state.astype(jnp.bfloat16)
        dstate = ds_ref[:, sl]
        dstateb = dstate.astype(jnp.bfloat16)
        into = eexp[:, sl]
        dec = dexp[:, sl]
        none = jnp.zeros_like(stateb)
        both = jnp.concatenate(
            [jnp.concatenate([stateb, none], axis=1), jnp.concatenate([none, dstateb], axis=1)]
        )
        product = dot(cbmat, both)
        carried = product[:, :LANES] * into
        bds = product[:, LANES:] * dec
        edy = (dy * into).astype(jnp.bfloat16)
        pulled = jnp.concatenate([edy, (xsf * dec).astype(jnp.bfloat16)], axis=1)
        dcb_ref[...] += dot_nt(pulled, both)
        tails = xsf * bds
        ends = jnp.sum(tails, axis=0, keepdims=True) + into[chunk - 1 : chunk, :] * jnp.sum(
            dstate * state, axis=0, keepdims=True
        )
        rowq = dy * (inner + carried) - xsf * dinner - tails + jnp.where(last_row, ends, 0.0)
        dxsum = dinner + bds
        row = lax.broadcasted_iota(jnp.int32, (LANES, LANES), 0)
        col = lax.broadcasted_iota(jnp.int32, (LANES, LANES), 1)
        gather = (col == 2 * p + row // HEAD).astype(jnp.bfloat16)
        aside = (col == HEAD + 2 * p + row // HEAD).astype(jnp.bfloat16)
        hi, mid, lo = split3(rowq)
        steps_hi = (xact * dxsum).astype(jnp.bfloat16)
        dcum_ref[...] += dot(
            jnp.concatenate([hi, mid], axis=1), jnp.concatenate([gather, gather])
        ) + dot(jnp.concatenate([lo, steps_hi], axis=1), jnp.concatenate([gather, aside]))
        ds_ref[:, sl] = dstate * into[chunk - 1 : chunk, :] + dot_tn(cmat, edy)
        acc_ref[5:6, sl] += jnp.sum(dy * xact, axis=0, keepdims=True)
        dact = sx * dxsum + cw[5:6, :] * dy
        dpre = dact * (sig * (1.0 + pre * (1.0 - sig)))
        grad = conv_back(dpre, cw, masks, here, back, dpad, tx_ref, sl, chunk, acc_ref)
        gproj_ref[:, pl.ds(pl.multiple_of(width + start, LANES), LANES)] = grad.astype(jnp.bfloat16)
        return carry

    lax.fori_loop(0, width // LANES, pair, 0, unroll=4)
    dgb = dg_ref[...].astype(jnp.bfloat16)
    grads = (dcb_ref[:, N:] + dot_tn(dgb, cmat), dcb_ref[:, :N] + dot(dgb, bmat))
    for half in range(2):
        sl = slice(half * LANES, (half + 1) * LANES)
        cw = cbc_ref[:, sl]
        pre, back, here = conv_parts(bpad, sl, chunk, cw, masks)
        sig = sigmoid(pre)
        dpre = grads[half] * (sig * (1.0 + pre * (1.0 - sig)))
        grad = conv_back(dpre, cw, masks, here, back, dpad, tbc_ref, sl, chunk, accbc_ref)
        at = 2 * width + half * LANES
        gproj_ref[:, at : at + LANES] = grad.astype(jnp.bfloat16)
    row = lax.broadcasted_iota(jnp.int32, (chunk, chunk), 0)
    col = lax.broadcasted_iota(jnp.int32, (chunk, chunk), 1)
    upper = (col >= row).astype(jnp.bfloat16)
    found = dcum_ref[...]
    below = lax.broadcasted_iota(jnp.int32, found.shape, 1) < HEAD
    dlogs = exact_left(upper, jnp.where(below, found, 0.0))
    direct = jnp.where(below, pltpu.roll(found, HEAD, 1), 0.0)
    dsteps = direct + dlogs * hp_ref[1:2, :]
    draw = dsteps * sigmoid(raw)
    gproj_ref[:, 2 * width + 256 :] = draw.astype(jnp.bfloat16)
    acch_ref[0:1, :] += jnp.sum(draw, axis=0, keepdims=True)
    acch_ref[1:2, :] += jnp.sum(dlogs * steps, axis=0, keepdims=True)


def mixer_backward(perm, proj, prior, meta, segrow, cw, cbc, hp, mix, up, fs, states, dstate, tx, tbc, chunk=CHUNK):
    rows, cols = proj.shape
    width = cw.shape[1]
    count = rows // chunk
    back = lambda c: count - 1 - c
    bc_at = 2 * width // 256
    f32 = jnp.float32
    per = chunk // 16
    ending = last_rows(count, chunk)

    def before(c, perm):
        return (perm[jnp.maximum(back(c) - 1, 0)] + 1) * per - 1

    return pl.pallas_call(
        backward_kernel,
        grid_spec=pltpu.PrefetchScalarGridSpec(
        num_scalar_prefetch=1,
        grid=(count,),
        in_specs=common_specs(chunk, width, back)
        + [
            pl.BlockSpec((16, width), lambda c, perm: (before(c, perm), 1)),
            pl.BlockSpec((16, 256), lambda c, perm: (before(c, perm), bc_at)),
            pl.BlockSpec((16, width), lambda c, perm: (ending(perm), 1)),
            pl.BlockSpec((16, 256), lambda c, perm: (ending(perm), bc_at)),
            pl.BlockSpec((chunk, 8), lambda c, perm: (back(c), 0)),
            pl.BlockSpec((1, 1, chunk), lambda c, perm: (back(c), 0, 0)),
            fixed((8, width)),
            fixed((8, 256)),
            fixed((8, LANES)),
            pl.BlockSpec((chunk, width), lambda c, perm: (perm[back(c)], 0)),
            pl.BlockSpec((chunk, width), lambda c, perm: (perm[back(c)], 0)),
            pl.BlockSpec((chunk, 8), lambda c, perm: (perm[back(c)], 0)),
            pl.BlockSpec((1, N, width), lambda c, perm: (back(c), 0, 0)),
            fixed((N, width)),
            fixed((3, 8, width)),
            fixed((3, 8, 256)),
        ],
        out_specs=[
            pl.BlockSpec((chunk, cols), lambda c, perm: (perm[back(c)], 0)),
            fixed((8, width)),
            fixed((8, 256)),
            fixed((8, LANES)),
            fixed((N, width)),
            fixed((3, 8, width)),
            fixed((3, 8, 256)),
        ],
        scratch_shapes=[
            pltpu.VMEM((chunk + 8, width), f32),
            pltpu.VMEM((chunk + 8, 256), f32),
            pltpu.VMEM((3, chunk, LANES), f32),
            pltpu.VMEM((chunk, 2 * width), f32),
            pltpu.VMEM((LANES, chunk), f32),
            pltpu.VMEM((chunk, chunk), f32),
            pltpu.VMEM((chunk, width), f32),
            pltpu.VMEM((chunk, width), f32),
            pltpu.VMEM((chunk, width), f32),
            pltpu.VMEM((LANES, width), jnp.bfloat16),
            pltpu.VMEM((LANES, 2 * width), jnp.bfloat16),
            pltpu.VMEM((chunk, chunk), f32),
            pltpu.VMEM((chunk, chunk), f32),
            pltpu.VMEM((chunk, 2 * N), f32),
            pltpu.VMEM((chunk, LANES), f32),
            pltpu.VMEM((3, chunk + 8, LANES), f32),
            pltpu.VMEM((chunk, LANES), f32),
            pltpu.VMEM((chunk, LANES), f32),
        ],
        ),
        out_shape=[
            jax.ShapeDtypeStruct((rows, cols), jnp.bfloat16),
            jax.ShapeDtypeStruct((8, width), f32),
            jax.ShapeDtypeStruct((8, 256), f32),
            jax.ShapeDtypeStruct((8, LANES), f32),
            jax.ShapeDtypeStruct((N, width), f32),
            jax.ShapeDtypeStruct((3, 8, width), f32),
            jax.ShapeDtypeStruct((3, 8, 256), f32),
        ],
        compiler_params=pltpu.CompilerParams(
            vmem_limit_bytes=VMEM_BYTES, dimension_semantics=("arbitrary",)
        ),
        cost_estimate=pl.CostEstimate(
            flops=rows * width * 56000, bytes_accessed=rows * width * 24, transcendentals=rows * width * 8
        ),
        name="mix_bwd",
    )(
        perm, proj, proj, proj, proj, proj, proj, prior, prior, meta, segrow, cw, cbc, hp,
        mix, up, fs, states, dstate, tx, tbc,
    )


def token_facts(seg, chunk=CHUNK):
    total = seg.shape[0]
    place = jnp.arange(total, dtype=jnp.int32)
    cols = []
    for m in (1, 2, 3):
        before = jnp.concatenate([jnp.full((m,), -1, jnp.int32), seg[:-m]])
        cols.append(before == seg)
    ends = seg.reshape(-1, chunk)[:, -1]
    starts = jnp.concatenate([jnp.full((1,), -1, jnp.int32), ends[:-1]])
    cols.append(jnp.repeat(starts, chunk) == seg)
    cols.append(jnp.repeat(ends, chunk) == seg)
    meta = jnp.stack([c.astype(jnp.float32) for c in cols] + [seg.astype(jnp.float32)], axis=1)
    meta = jnp.pad(meta, ((0, 0), (0, 2)))
    return meta, seg.astype(jnp.float32).reshape(-1, 1, chunk)


def swap(value, axis):
    return lax.ppermute(value, axis, SWAP)


def paired():
    return lax.axis_size("x") == 2


def member_index():
    return lax.axis_index("core") * lax.axis_size("x") + lax.axis_index("x")


def slot_of(members):
    return members ^ member_index() if paired() else members


def team_gather(own, *first):
    if paired():
        came = swap(own, "x")
        row = after(jnp.concatenate([own, came]), *first)
        return jnp.concatenate([row, swap(row, "core")]), came
    row = lax.all_gather(own, "x", axis=0, tiled=True)
    other = swap(row, "core")
    first = lax.axis_index("core") == 0
    return jnp.concatenate([jnp.where(first, row, other), jnp.where(first, other, row)]), row


def team_reduce(blocks, rows, kind, first=()):
    half = lax.axis_size("x") * rows
    if paired():
        got = swap(blocks[half:], "core")
        near = blocks[rows:half].astype(jnp.float32) + got[rows:].astype(jnp.float32)
        near = after(near.astype(kind), *first)
        far = swap(near, "x")
        total = blocks[:rows].astype(jnp.float32) + got[:rows].astype(jnp.float32)
        return total + far.astype(jnp.float32), near, far
    core = lax.axis_index("core")
    halves = blocks.reshape((2, half) + blocks.shape[1:])
    got = swap(lax.dynamic_index_in_dim(halves, 1 - core, 0, False), "core")
    keep = lax.dynamic_index_in_dim(halves, core, 0, False)
    sums = (keep.astype(jnp.float32) + got.astype(jnp.float32)).astype(kind)
    total = lax.psum_scatter(sums, "x", scatter_dimension=0, tiled=True)
    return total.astype(jnp.float32), sums, total


def plane_cycle():
    across = lax.axis_size("y")
    walk = [0]
    for y in range(across):
        line = range(1, DEPTH) if y % 2 == 0 else range(DEPTH - 1, 0, -1)
        walk += [y * DEPTH + z for z in line]
    return walk + [y * DEPTH for y in range(across - 1, 0, -1)]


def plane_steps():
    walk = plane_cycle()
    count = len(walk)
    places = [walk.index(i) for i in range(count)]
    here = jnp.asarray(places, jnp.int32)[lax.axis_index("y") * DEPTH + lax.axis_index("z")]
    forwards = [(walk[i], walk[(i + 1) % count]) for i in range(count)]
    return jnp.asarray(walk, jnp.int32), here, forwards, [(b, a) for a, b in forwards]


def ring_gather(block, beside=()):
    walk, here, forwards, backwards = plane_steps()
    count = walk.shape[0]
    rows = block.shape[0]

    def put(whole, value, place):
        return lax.dynamic_update_slice_in_dim(whole, value, walk[place % count] * rows, 0)

    whole = put(jnp.zeros((count * rows, block.shape[1]), block.dtype), block, here)
    ahead = behind = block
    for step in range(1, count // 2 + 1):
        ahead = lax.ppermute(ahead, ("y", "z"), forwards)
        whole = put(whole, ahead, here + count - step)
        if step < count - count // 2:
            behind = lax.ppermute(behind, ("y", "z"), backwards)
            whole = put(whole, behind, here + step)
        if step <= len(beside):
            ahead = after(ahead, beside[step - 1])
    return whole


def deal_moves():
    moves = []
    for r in range(2):
        pairs = []
        for core in range(2):
            for z in range(DEPTH):
                pairs.append((core * DEPTH + z, (z // 2) * DEPTH + 2 * core + ((z % 2) ^ r)))
        moves.append(pairs)
    return moves


def column_blocks(across, rows):
    wide = lax.axis_size("x") * rows
    for y in range(across):
        for core in range(2):
            for z in range(DEPTH):
                yield ((y * DEPTH + z) * 2 + core) * wide, ((y * 2 + core) * DEPTH + z) * wide, wide


def to_team(rows, weight_rows):
    blocks = list(column_blocks(lax.axis_size("y"), weight_rows))
    low = lax.axis_index("z") % 2

    def body(low_ref, rows_ref, *out_refs):
        for to, at, wide in blocks:
            for r in range(2):
                out_refs[r][:, to : to + wide] = rows_ref[low_ref[0] ^ r, :, at : at + wide]

    shape = jax.ShapeDtypeStruct(rows.shape[1:], rows.dtype)
    sent = pl.pallas_call(
        body,
        grid_spec=pltpu.PrefetchScalarGridSpec(
            num_scalar_prefetch=1,
            grid=(1,),
            in_specs=[pl.BlockSpec(rows.shape, lambda c, low: (0, 0, 0))],
            out_specs=[pl.BlockSpec(rows.shape[1:], lambda c, low: (0, 0))] * 2,
        ),
        out_shape=[shape, shape],
        compiler_params=pltpu.CompilerParams(vmem_limit_bytes=VMEM_BYTES),
        name="to_plane",
    )(low.reshape(1), rows)
    return [lax.ppermute(v, ("core", "z"), pairs) for v, pairs in zip(sent, deal_moves())]


def from_team(rows):
    moves = zip(rows, deal_moves())
    return [lax.ppermute(v, ("core", "z"), [(b, a) for a, b in pairs]) for v, pairs in moves]


def dealt(got, weight_rows, kind):
    blocks = list(column_blocks(lax.axis_size("y"), weight_rows))
    low = lax.axis_index("z") % 2
    shape = got[0].shape

    def body(low_ref, first_ref, second_ref, out_ref):
        for at, to, wide in blocks:
            for r, ref in enumerate((first_ref, second_ref)):
                out_ref[low_ref[0] ^ r, :, to : to + wide] = ref[:, at : at + wide].astype(kind)

    return pl.pallas_call(
        body,
        grid_spec=pltpu.PrefetchScalarGridSpec(
            num_scalar_prefetch=1,
            grid=(1,),
            in_specs=[pl.BlockSpec(shape, lambda c, low: (0, 0))] * 2,
            out_specs=pl.BlockSpec((2,) + shape, lambda c, low: (0, 0, 0)),
        ),
        out_shape=jax.ShapeDtypeStruct((2,) + shape, kind),
        compiler_params=pltpu.CompilerParams(vmem_limit_bytes=VMEM_BYTES),
        name="to_natural",
    )(low.reshape(1), *got)


def inverse_of(perm):
    count = perm.shape[0]
    places = jnp.arange(count, dtype=jnp.int32)
    return jnp.sum(jnp.where(places[:, None] == perm[None, :], places[None, :], 0), axis=1)


def segments_of(sizes, total):
    ends = jnp.cumsum(sizes)
    places = jnp.arange(total, dtype=jnp.int32)
    return jnp.sum((places[:, None] >= ends[None, :]).astype(jnp.int32), axis=1)


def reorder(values, axis, inner, outer):
    shape = values.shape
    count = lax.axis_size("y")
    view = values.reshape(shape[:axis] + (count, inner, outer, -1) + shape[axis + 1 :])
    order = list(range(view.ndim))
    order[axis + 1], order[axis + 2] = axis + 2, axis + 1
    return view.transpose(order).reshape(shape)


def to_plane(values, axis):
    return reorder(values, axis, 2, DEPTH)


def to_members(pieces):
    sent = lax.all_to_all(pieces, ("core", "x"), split_axis=1, concat_axis=0, tiled=True)
    return sent.reshape(-1, pieces.shape[2])


def plane_gather(block):
    return lax.all_gather(block, ("y", "z"), axis=0, tiled=True)


def from_plane(summed):
    team = 2 * lax.axis_size("x")
    blocks = summed.reshape(team, -1, summed.shape[1])
    return lax.all_to_all(blocks, ("core", "x"), split_axis=0, concat_axis=0, tiled=True)


def after(value, *others):
    return lax.optimization_barrier((value,) + others)[0]


def in_kernel(layers, team, width, split_refs, weight_ref, grad_ref, norm_ref, tile_ref):
    for layer in range(layers):
        total = jnp.zeros(norm_ref.shape[1:], jnp.float32)
        pieces = []
        for q in range(team):
            pieces.append((q * width, split_refs[layer][q, :, :width].astype(jnp.float32)))
            pieces.append((DI + q * width, split_refs[layer][q, :, width : 2 * width].astype(jnp.float32)))
        states = split_refs[layer][0, :, 2 * width : 2 * width + 2 * N].astype(jnp.float32)
        for q in range(1, team):
            states = states + split_refs[layer][q, :, 2 * width : 2 * width + 2 * N].astype(jnp.float32)
        pieces.append((2 * DI, states))
        for at, value in pieces:
            count = value.shape[1]
            grad_ref[layer, :, at : at + count] = value
            product = value * weight_ref[layer, :, at : at + count].astype(jnp.float32)
            for tile in range(count // LANES):
                total = total + product[:, tile * LANES : (tile + 1) * LANES]
        tiles = split_refs[layer][:, :, 2 * width + 2 * N :].astype(jnp.float32)
        tile_ref[layer] = tiles
        count = (weight_ref.shape[2] - 2 * DI - 2 * N) // team
        steps = jnp.zeros(norm_ref.shape[1:], jnp.float32)
        lane = lax.broadcasted_iota(jnp.int32, steps.shape, 1)
        for q in range(team):
            moved = pltpu.roll(tiles[q], q * count, 1) if q else tiles[q]
            steps = jnp.where((lane >= q * count) & (lane < (q + 1) * count), moved, steps)
        grad_ref[layer, :, 2 * DI + 2 * N :] = steps[:, : team * count]
        product = steps[:, : team * count] * weight_ref[layer, :, 2 * DI + 2 * N :].astype(jnp.float32)
        norm_ref[layer] = jnp.broadcast_to(
            jnp.sum(total, axis=1, keepdims=True) + jnp.sum(product, axis=1, keepdims=True), total.shape
        )


def assemble_in(splits, in_weight):
    layers, rows, cols = in_weight.shape
    team, width = splits[0].shape[0], DI // splits[0].shape[0]

    def body(*refs):
        in_kernel(layers, team, width, refs[:layers], *refs[layers:])

    return pl.pallas_call(
        body,
        out_shape=[
            jax.ShapeDtypeStruct((layers, rows, cols), jnp.float32),
            jax.ShapeDtypeStruct((layers, rows, LANES), jnp.float32),
            jax.ShapeDtypeStruct((layers, team, rows, LANES), jnp.float32),
        ],
        compiler_params=pltpu.CompilerParams(vmem_limit_bytes=VMEM_BYTES),
        name="grad_in",
    )(*splits, in_weight)


def assemble_out(outs):
    layers = len(outs)
    team, rows, width = outs[0].shape

    def body(*refs):
        for layer in range(layers):
            for q in range(team):
                refs[layers][layer, :, q * width : (q + 1) * width] = refs[layer][q].astype(jnp.float32)

    return pl.pallas_call(
        body,
        out_shape=jax.ShapeDtypeStruct((layers, rows, DI), jnp.float32),
        compiler_params=pltpu.CompilerParams(vmem_limit_bytes=VMEM_BYTES),
        name="grad_out",
    )(*outs)


def in_columns(w_in, team, extra):
    rows = w_in.shape[0]
    bc = w_in[:, 2 * DI : 2 * DI + 2 * N]
    step = w_in[:, 2 * DI + 2 * N :].reshape(rows, team, -1)
    shared = jnp.concatenate(
        [extra, jnp.zeros((rows, LANES - step.shape[2] - extra.shape[1]), w_in.dtype)], axis=1
    )
    return jnp.concatenate(
        [
            w_in[:, :DI].reshape(rows, team, -1),
            w_in[:, DI : 2 * DI].reshape(rows, team, -1),
            jnp.broadcast_to(bc[:, None, :], (rows, team, 2 * N)),
            step,
            jnp.broadcast_to(shared[:, None, :], (rows, team, shared.shape[1])),
        ],
        axis=2,
    )


def rounded(values):
    return lax.reduce_precision(values, 8, 7)


def in_parts(values):
    hi = rounded(values)
    mid = rounded(values - hi)
    return jnp.stack([hi, mid, rounded(values - hi - mid)]).astype(jnp.bfloat16)


def as_rows(flat, rows):
    count = -(-flat.shape[-1] // rows)
    flat = jnp.pad(flat, [(0, 0)] * (flat.ndim - 1) + [(0, count * rows - flat.shape[-1])])
    return jnp.swapaxes(flat.reshape(flat.shape[:-1] + (count, rows)), -1, -2)


def row_scale(rows):
    return lax.rsqrt(jnp.mean(rows * rows, axis=1, keepdims=True) + EPS)


def per_device(
    hidden,
    lengths,
    token_order,
    norm_gain,
    in_weight,
    conv_weight,
    conv_bias,
    dt_bias,
    log_decay,
    skip_gain,
    gate_gain,
    out_weight,
    cotangent,
):
    bf16, f32 = jnp.bfloat16, jnp.float32
    layers = in_weight.shape[0]
    across = lax.axis_size("x")
    team = 2 * across
    core, z, x = (lax.axis_index(name) for name in ("core", "z", "x"))
    member = member_index()
    width = DI // team
    heads = width // HEAD
    rows_here = hidden.shape[1]
    tokens = token_order.shape[2]
    part_rows = tokens // PARTS
    own_rows = part_rows // team
    weight_rows = in_weight.shape[1]
    wide = conv_bias.shape[1]
    gate_wide = gate_gain.shape[1]
    head_wide = dt_bias.shape[1]
    bc_at = 2 * width
    step_at = bc_at + 2 * N
    extra_at = step_at + heads
    numbers = jnp.arange(tokens, dtype=jnp.int32)

    def of_pair(ints):
        return lax.dynamic_index_in_dim(
            jnp.where(z // 2 == core, ints, swap(ints, "core")), z % 2, 0, False
        )[0]

    order, sizes = of_pair(token_order), of_pair(lengths)
    inverse = inverse_of(order)
    mine = z % 2
    block, within = inverse // rows_here, inverse % rows_here
    from_z, from_x = block // across, block % across
    place = (slot_of(from_z // 2 * across + from_x) * 2 + (from_z % 2 ^ mine)) * rows_here + within
    if paired():
        view = place.reshape(PARTS, 2, 2, own_rows)
        view = jnp.where(core == 1, view[:, ::-1], view)
        place = jnp.where(x == 1, view[:, :, ::-1], view).reshape(-1)
    target = jnp.concatenate(
        [
            lax.dynamic_slice_in_dim(order, ((2 * core + (r ^ mine)) * across + x) * rows_here, rows_here)
            for r in range(2)
        ]
    )
    inside = target % part_rows
    own_place = (
        target // part_rows * part_rows + slot_of(inside // own_rows) * own_rows + inside % own_rows
    )
    meta, segrow = token_facts(segments_of(sizes, tokens))
    chunks = numbers[: part_rows // CHUNK]
    if paired():
        per = own_rows // CHUNK
        perm = slot_of(chunks // per) * per + chunks % per
    else:
        perm = chunks

    small = []
    for layer in range(layers):
        per_head = jnp.stack([dt_bias[layer], log_decay[layer], skip_gain[layer]])
        flat = [conv_weight[layer], conv_bias[layer], gate_gain[layer], in_parts(per_head)]
        flat = as_rows(jnp.concatenate([v.reshape(-1) for v in flat]), weight_rows)
        small.append(jnp.concatenate([norm_gain[layer][:, None], flat], axis=1))
    extras = small[0].shape[1]
    def part(values, i):
        return values[i * part_rows : (i + 1) * part_rows]

    places = [part(place, i) for i in range(PARTS)]
    arrived = to_team(hidden, weight_rows)
    sent_in = to_members(in_columns(in_weight[0], team, small[0]))
    pieces = [out_weight[layer].T.reshape(-1, team, width) for layer in range(layers)]
    pieces += [in_columns(in_weight[layer], team, small[layer]) for layer in range(1, layers)]
    blocks = to_members(after(jnp.concatenate(pieces, axis=2), sent_in))
    gathered, came = team_gather(jnp.concatenate(arrived))
    w_cols = [ring_gather(sent_in, (blocks, came, gathered))]
    everything = [gathered[at] for at in places]
    w_out = [plane_gather(blocks[:, :width])]
    arrived_out = to_team(after(cotangent, everything[0]), weight_rows)
    gout_gathered, came_out = team_gather(jnp.concatenate(arrived_out))
    cols = sent_in.shape[1]
    for layer in range(1, layers):
        start = layers * width + (layer - 1) * cols
        w_cols.append(plane_gather(after(blocks[:, start : start + cols], gathered)))
        block = blocks[:, layer * width : (layer + 1) * width]
        w_out.append(plane_gather(after(block, everything[0])))

    def own_columns(values):
        return lax.dynamic_slice_in_dim(values, member * width, width, values.ndim - 1)

    def tables_of(tile):
        spare = tile.astype(f32).T[heads : heads + extras]
        gain = spare[0]
        flat = spare[1:].reshape(extras - 1, -1, weight_rows).transpose(1, 0, 2)
        flat = flat.reshape(-1, DEPTH, 2, across, weight_rows * (extras - 1))
        heads_flat = flat[0, :, 0, :, (CONV + 1) * wide + gate_wide :][:, :, : 9 * head_wide]
        per_head = jnp.sum(heads_flat.astype(f32).reshape(-1, 3, 3, head_wide), axis=1)
        per_head = per_head.transpose(1, 0, 2).reshape(3, -1)
        own_heads = lax.dynamic_slice_in_dim(per_head, member * heads, heads, 1)
        flat = flat.transpose(0, 2, 1, 3, 4).reshape(-1, weight_rows * (extras - 1)).astype(f32)
        taps = flat[:, : CONV * wide].reshape(-1, CONV, wide).transpose(1, 0, 2).reshape(CONV, -1)
        shift = flat[:, CONV * wide : (CONV + 1) * wide].reshape(1, -1)
        ggain = flat[:, (CONV + 1) * wide : (CONV + 1) * wide + gate_wide].reshape(1, -1)
        cw = jnp.concatenate(
            [
                own_columns(taps[:, :DI]),
                own_columns(shift[:, :DI]),
                jnp.repeat(own_heads[2], HEAD)[None],
                own_columns(ggain),
                jnp.zeros((1, width), f32),
            ]
        )
        cbc = jnp.concatenate([taps[:, DI:], shift[:, DI:], jnp.zeros((3, 2 * N), f32)])
        hp = jnp.stack([own_heads[0], -jnp.exp(own_heads[1])])
        return gain, (cw, cbc, jnp.pad(hp, ((0, 6), (0, LANES - heads))))

    def facts(i):
        count = part_rows // CHUNK
        return part(meta, i), segrow[i * count : (i + 1) * count]

    def own_first(values):
        start = 0 if paired() else member * own_rows
        return lax.dynamic_slice_in_dim(values, start, own_rows, 0)

    states = [own_first(everything[i]).astype(f32) for i in range(PARTS)]
    record = []
    last = []

    def turn(value, *needed):
        return after(value, *last, *needed)

    def done(value):
        last[:] = [value]
        return value

    ready, needed = tuple(arrived_out), ()
    tables, gains, own_normed, gathered_rows = [], [], [None] * PARTS, [None] * PARTS

    def normed_rows(rows, gain, *before):
        rows = after(rows, *before)
        return (rows * row_scale(rows) * gain).astype(bf16)

    for layer in range(layers):
        gain, table = tables_of(turn(w_cols[layer][:, step_at:]))
        gains.append(gain)
        tables.append(table)
        kept = []
        state = jnp.zeros((N, width), f32)
        before = None
        for i in range(PARTS):
            rows = states[i]
            if layer == 0:
                every = everything[i].astype(f32)
                normed = (every * row_scale(every) * gain).astype(bf16)
            else:
                normed = gathered_rows[i]
            proj = jnp.dot(turn(normed), w_cols[layer], preferred_element_type=f32).astype(bf16)
            done(proj)
            before = proj if before is None else before
            mix, gated, squares, starts, state = mixer_forward(
                perm, turn(proj, *ready), before, *facts(i), *table, state
            )
            done(gated)
            partial = done(dot_nt(turn(gated, *needed), w_out[layer]).astype(bf16))
            total, sent_total, far_total = team_reduce(jnp.sum(squares, axis=1), own_rows, f32)
            branch, sent, far = team_reduce(partial, own_rows, bf16, (far_total,))
            factor = lax.rsqrt(total / DI + EPS)
            states[i] = rows + branch * factor[:, None]
            ready, needed = (sent,), (far,)
            if layer + 1 < layers:
                later = tables_of(w_cols[layer + 1][:, step_at:])[0]
                own_normed[i] = normed_rows(states[i], later, *own_normed[:i])
                gathered_rows[i], _ = team_gather(own_normed[i])
                needed = (own_normed[i],)
            if layer == 0 and i == 0:
                ready += (came_out,)
            if layer == 0 and i == PARTS - 1:
                rows_at = turn(gout_gathered)
                gout_parts = [rows_at[at] for at in places]
                ready += tuple(gout_parts)
            kept.append((rows, normed, proj, before, mix, starts, branch.astype(bf16), factor, gated))
            before = proj
        record.append(kept)

    def with_small(sum_in, sums, layer):
        acc, acc_bc, acc_h = sums
        taps_full = jnp.zeros((CONV + 1, DI + 2 * N), f32)
        taps_full = lax.dynamic_update_slice(taps_full, acc[: CONV + 1], (0, member * width))
        taps_full = lax.dynamic_update_slice(taps_full, acc_bc[: CONV + 1], (0, DI))
        gate_full = lax.dynamic_update_slice(jnp.zeros((DI,), f32), acc[6], (member * width,))
        head_sums = jnp.stack(
            [
                acc_h[0, :heads],
                acc_h[1, :heads] * tables[layer][2][1, :heads],
                jnp.sum(acc[5].reshape(heads, HEAD), axis=1),
            ]
        )
        head_full = lax.dynamic_update_slice(
            jnp.zeros((3, team * heads), f32), head_sums, (0, member * heads)
        )
        head_full = head_full.reshape(3, -1, head_wide).transpose(1, 0, 2).reshape(-1, 3 * head_wide)
        owners = 2 * lax.axis_size("y")
        flat = jnp.concatenate(
            [
                taps_full.reshape(CONV + 1, -1, wide).transpose(1, 0, 2).reshape(-1, (CONV + 1) * wide),
                gate_full.reshape(-1, gate_wide),
                jnp.tile(head_full, (owners, 1)),
            ],
            axis=1,
        )
        flat = as_rows(to_plane(flat, 0), weight_rows)
        spare = flat.shape[-1]
        flat = flat.reshape(-1, spare).astype(bf16)
        tile = jnp.concatenate(
            [
                sum_in[:, step_at:extra_at],
                flat,
                jnp.zeros((flat.shape[0], LANES - heads - spare), bf16),
            ],
            axis=1,
        )
        return lax.dynamic_update_slice(sum_in, tile, (0, step_at))

    def picked(parts):
        return jnp.concatenate(parts)[own_place].reshape(2, rows_here, -1)

    grads_rows = [own_first(gout_parts[i]).astype(f32) for i in range(PARTS)]

    def gather_rows(values):
        return team_gather(values[None])[0].reshape(part_rows)

    factors = [[gather_rows(record[layer][i][7]) for i in range(PARTS)] for layer in range(layers)]

    def scales_of(layer, i):
        branch, factor = record[layer][i][6:8]
        inner = jnp.sum(grads_rows[i].astype(bf16).astype(f32) * branch.astype(f32), axis=1)
        pulls = gather_rows(factor * factor * factor * inner / DI)
        return jnp.pad(jnp.stack([factors[layer][i], pulls], axis=1), ((0, 0), (0, 6)))

    def pull_in(layer, i, gout, scales, *needed):
        up = done(jnp.dot(turn(gout), w_out[layer], preferred_element_type=f32).astype(bf16))
        rows, normed, proj, before, mix, starts = record[layer][i][:6]
        found = mixer_backward(
            perm, proj, before, *facts(i), *tables[layer], mix, turn(up, *needed), scales, starts, *carry[0]
        )
        done(found[0])
        carry[0] = found[4:]
        carry[1] = found[1:4] if carry[1] is None else tuple(a + b for a, b in zip(carry[1], found[1:4]))
        return found[0]

    def send_back(layer, gproj, *needed):
        partial = done(dot_nt(turn(gproj, *needed), w_cols[layer]).astype(bf16))
        return team_reduce(partial, own_rows, bf16)

    def add_in(layer, i, gproj, total, *needed):
        term = dot_tn(record[layer][i][1], turn(gproj, *needed))
        return done((term if total is None else term + total.astype(f32)).astype(bf16))

    def add_out(layer, i, gout, total, *needed):
        scaled = record[layer][i][8].astype(f32) * factors[layer][i][:, None]
        term = dot_tn(turn(gout, *needed), scaled.astype(bf16))
        return done((term if total is None else term + total.astype(f32)).astype(bf16))

    def step_back(layer, i, gnormed):
        rows = record[layer][i][0]
        scale = row_scale(rows)
        pulled = gnormed * gains[layer]
        back = jnp.mean(pulled * rows, axis=1, keepdims=True)
        return grads_rows[i] + scale * pulled - rows * (scale * scale * scale * back)

    def plane_sum(values):
        return lax.psum_scatter(values, ("y", "z"), scatter_dimension=0, tiled=True)

    carry = [None, None]
    splits, outs = [None] * layers, [None] * layers
    gouts = list(gout_parts)
    top = layers - 1
    sum_out = None
    for i in reversed(range(PARTS)):
        sum_out = add_out(top, i, gouts[i], sum_out)
    sum_out_done = plane_sum(sum_out)
    outs[top] = from_plane(sum_out_done)
    scales = [scales_of(top, i) for i in range(PARTS)]
    sent, pending = (), None
    out_parts = [None] * PARTS

    def catch_up(pending, *started):
        layer, i, gnormed = pending
        grads_rows[i] = step_back(layer, i, after(gnormed, *started))
        own = grads_rows[i].astype(bf16)
        if layer > 0:
            next_gouts[i] = team_gather(own)
            next_scales[i] = scales_of(layer - 1, i)
        else:
            last_rows_of[i] = team_gather(own)
        return (own,)

    last_rows_of = [None] * PARTS
    next_gouts, next_scales = gouts, scales
    for layer in reversed(range(layers)):
        carry[:] = [
            (jnp.zeros((N, width), f32), jnp.zeros((3, 8, width), f32), jnp.zeros((3, 8, 2 * N), f32)),
            None,
        ]
        sum_in, sum_out, kept = None, None, [None] * PARTS
        if layer == top:
            next_gouts, next_scales = [None] * PARTS, [None] * PARTS
        for i in reversed(range(PARTS)):
            if layer < top:
                gouts[i], scales[i] = next_gouts[i][0], next_scales[i]
            gproj = pull_in(layer, i, gouts[i], scales[i], *sent)
            kept[i] = gproj
            needed = catch_up(pending, gproj) if pending is not None else ()
            if layer == top:
                out_parts[i], came = team_gather(after(states[i].astype(bf16), gproj))
                if i + 1 < PARTS:
                    needed += (out_parts[i + 1],)
            if layer == top - 1 and i == PARTS - 1:
                needed += (sum_out_done,)
            if layer == 0 and i == 0:
                needed += (out_parts[0],)
                sum_in = add_in(layer, i, gproj, sum_in, *needed, *splits[1:], *outs[1:])
                sum_in = done(with_small(sum_in, carry[1], layer))
                splits[layer] = plane_sum(sum_in)
            gnormed, near, far = send_back(layer, gproj, *needed)
            sent, pending = (near,), (layer, i, gnormed)
            if layer == 0 and i > 0:
                sum_out = add_out(layer, i, gouts[i], sum_out)
                sum_in = add_in(layer, i, gproj, sum_in, next_gouts[i - 1][1])
                sum_out = add_out(layer, i - 1, next_gouts[i - 1][0], sum_out)
                summed_out = plane_sum(sum_out)
        if layer > 0:
            for i in reversed(range(PARTS)):
                wait = next_gouts[i + 1][1:] if i + 1 < PARTS else ()
                sum_in = add_in(layer, i, kept[i], sum_in, *wait)
            sum_in = done(with_small(sum_in, carry[1], layer))
            splits[layer] = from_plane(plane_sum(sum_in))
        else:
            outs[layer] = from_plane(summed_out)
    block_out = from_team(picked([after(p, *last) for p in out_parts]))
    catch_up(pending)
    rows = picked([p[0] for p in last_rows_of])
    block_out = dealt(block_out, weight_rows, bf16)
    grad_hidden = dealt(from_team(rows), weight_rows, f32)
    splits[0] = from_plane(after(splits[0], block_out, grad_hidden))
    grad_out = assemble_out(outs).transpose(0, 2, 1)
    grad_in, products, tiles = assemble_in(splits, in_weight)
    spare = extras - 1
    sums = jnp.sum(tiles, axis=1).transpose(0, 2, 1)[:, heads : heads + spare].reshape(layers, -1)
    shift_at, gate_at, head_at = CONV * wide, (CONV + 1) * wide, (CONV + 1) * wide + gate_wide
    grad_heads = sums[:, head_at : head_at + 3 * head_wide].reshape(layers, 3, head_wide)
    return (
        block_out,
        grad_hidden,
        products[:, :, 0] / norm_gain.astype(f32),
        grad_in,
        sums[:, :shift_at].reshape(layers, CONV, wide),
        sums[:, shift_at:gate_at],
        grad_heads[:, 0],
        grad_heads[:, 1],
        grad_heads[:, 2],
        sums[:, gate_at:head_at],
        grad_out,
    )


def solution(mesh):
    grid = mesh.devices.reshape(mesh.shape["dp"] // 2, 2, DEPTH, mesh.shape["seq"] // DEPTH)
    fine = Mesh(grid, ("y", "core", "z", "x"))
    dp, seq = ("y", "core"), ("z", "x")
    both = dp + seq
    return jax.shard_map(
        per_device,
        mesh=fine,
        in_specs=(
            P(None, both, None),
            P(None, dp, None),
            P(None, dp, None),
            P(None, both),
            P(None, both, None),
            P(None, None, both),
            P(None, both),
            P(None, seq),
            P(None, seq),
            P(None, seq),
            P(None, both),
            P(None, None, both),
            P(None, both, None),
        ),
        out_specs=(
            P(None, both, None),
            P(None, both, None),
            P(None, both),
            P(None, both, None),
            P(None, None, both),
            P(None, both),
            P(None, seq),
            P(None, seq),
            P(None, seq),
            P(None, both),
            P(None, None, both),
        ),
        check_vma=False,
    )
```
